256 devices in a mesh: section: 2 (over x_lo), seq: 16 (over z, x_hi), tp: 8 (over y, core).
Axes of the slice: x: 4 (x_hi: 2, x_lo: 2; x = x_hi * 2 + x_lo), y: 4, z: 8, core: 2. Of those that a mesh axis runs over, the one named last changes fastest.
Arguments:
- layer_input: bfloat16 [2, 4096, 8192], P('section', 'seq', 'tp'), may hold values from -200 to 200, as said below
- norm_gain: float32 [2, 8192], P('section', 'tp'), may hold values from 0.1 to 1.9
- kv_cotangent: bfloat16 [2, 4096, 2048], P('section', 'seq', 'tp'), may hold values from -8 to 8
- kv_weight: bfloat16 [2, 2048, 8192], P('section', 'tp', 'seq'), may hold values from -0.09375 to 0.09375
- mlp_grads: bfloat16 [2, 4096, 8192], P('section', 'seq', 'tp'), may hold values from -6 to 6
- output_cotangent: bfloat16 [4096, 8192], P('seq', 'tp'), may hold values from -6 to 6
- out_weight: bfloat16 [2, 8192, 8192], P('section', 'tp', 'seq'), may hold values from -0.0625 to 0.0625
Outputs:
- attn_grads: bfloat16 [2, 4096, 8192], P('section', 'seq', 'tp')
- input_grads: bfloat16 [2, 4096, 8192], P('section', 'seq', 'tp')
The draws below stay inside these ranges and needn't reach their ends.
Inputs may be any that keep to these rules, and one draw needn't show every extreme that they name: `layer_input`: real-valued activations.
All inputs are finite; a program needn't handle non-finite values.
Results may differ from the reference program's by a relative error of at most 0.0055.
Values may be sent and summed in bfloat16 or wider, within the bound.
A program may use at most 128 MiB of HBM per device.

```python
import math
import jax
import jax.numpy as jnp
from jax import lax

D = 8192
HH = 8192
KVW = 2048
TOKENS = 4096


def draw_layer_input(key, part):
    key = jax.random.fold_in(key, 17)
    key_base, key_row, key_col = jax.random.split(key, 3)
    position = jnp.arange(D, dtype=jnp.float32) / D
    col_scale = jnp.exp(jax.random.uniform(key_col, (2, 1, D), jnp.float32) * math.log(10.0))
    row_scale = jnp.exp(jax.random.uniform(key_row, (2, TOKENS, 1), jnp.float32) * math.log(10.0))
    base = jax.random.truncated_normal(key_base, -4.0, 4.0, (2, TOKENS, D), jnp.float32)
    rise = jnp.exp(position * 0.5 * math.log(3.0))
    return (0.1 * row_scale * col_scale * rise * base).astype(jnp.bfloat16)


def spiked(result, stream_key, source, target, shards_of, factor):
    def block_of(axis_at):
        return (jnp.arange(result.shape[axis_at]) // (result.shape[axis_at] // shards_of)).reshape((-1,) + (1,) * (result.ndim - 1 - axis_at))

    near = jax.random.permutation(stream_key, shards_of)[block_of(target)]
    second = (block_of(target) + shards_of // 2) % shards_of
    return jnp.where((block_of(source) == near) | (block_of(source) == second), factor * result, result)


def level_of(stream_key, dims, cuts, low, high):
    factor_of, own = 1.0, jax.random.fold_in(stream_key, 6)
    for dim, blocks in cuts:
        heights = jnp.exp(jax.random.uniform(jax.random.fold_in(own, dim), (blocks,), jnp.float32, low / len(cuts), high / len(cuts)))
        factor_of = factor_of * jnp.repeat(heights, dims[dim] // blocks).reshape([-1 if axis == dim else 1 for axis in range(len(dims))])
    return factor_of


def centred(key, dims, scale, bound, pieces=(), kind=jnp.bfloat16):
    values = jax.random.normal(key, dims, jnp.float32) * scale
    if len(pieces) > 0:
        values = level_of(key, dims, pieces, -0.22, 0.18) * values
    return jnp.clip(values, min=-bound, max=bound).astype(kind)


def noise_with(rng, extent, width, limit, pieces, heavy, held_as=jnp.bfloat16):
    array = width * jax.random.normal(rng, extent, jnp.float32)
    if pieces:
        array = array * level_of(rng, extent, pieces, -0.22, 0.18)
    return jnp.clip(spiked(array, jax.random.fold_in(rng, 3), *heavy), -limit, limit).astype(held_as)


def setup_inputs(seed: int = 0) -> dict:
    keys = jax.random.split(jax.random.key(seed), 8)
    return {
        "layer_input": draw_layer_input(jax.random.fold_in(keys[7], 71), 0),
        "norm_gain": jnp.clip(1.0 + 0.18 * jax.random.normal(keys[1], (2, D), jnp.float32), 0.1, 1.9),
        "kv_cotangent": centred(keys[2], (2, TOKENS, KVW), 2.0, 8.0, ((0, 2), (1, 16), (2, 8))),
        "kv_weight": noise_with(keys[3], (2, KVW, D), D ** -0.5, 0.09375, ((0, 2), (1, 8), (2, 16)), (1, 2, 16, 2.0)),
        "mlp_grads": centred(keys[4], (2, TOKENS, D), 1.0, 6.0, ((0, 2), (1, 16), (2, 8))),
        "output_cotangent": centred(keys[5], (TOKENS, D), 1.0, 6.0, ((0, 16), (1, 8))),
        "out_weight": centred(keys[6], (2, HH, D), HH ** -0.5, 0.0625, ((0, 2), (1, 8), (2, 16))),
    }


epsilon = 1e-05

def norm_backward(layer_input, norm_gain, kv_cotangent, kv_weight, slot):
    kv_terms = jnp.dot(kv_cotangent[slot], kv_weight[slot], preferred_element_type=jnp.float32)
    values = layer_input[slot].astype(jnp.float32)
    inv_rms = lax.rsqrt(lax.optimization_barrier(jnp.sum(values * values, axis=1, keepdims=True)) / D + epsilon)
    intersection = lax.optimization_barrier(jnp.sum(norm_gain[slot] * kv_terms * values, axis=1, keepdims=True))
    return inv_rms * norm_gain[slot] * kv_terms - values * (inv_rms * inv_rms * inv_rms) * intersection / D

def reference(layer_input, norm_gain, kv_cotangent, kv_weight, mlp_grads, output_cotangent, out_weight):
    back_one = norm_backward(layer_input, norm_gain, kv_cotangent, kv_weight, 1)
    back_zero = norm_backward(layer_input, norm_gain, kv_cotangent, kv_weight, 0)
    grad_one = output_cotangent.astype(jnp.float32) + mlp_grads[1].astype(jnp.float32)
    input_one = (grad_one + back_one).astype(jnp.bfloat16)
    grad_zero = input_one.astype(jnp.float32) + mlp_grads[0].astype(jnp.float32)
    input_zero = (grad_zero + back_zero).astype(jnp.bfloat16)
    attn_zero = jnp.dot(grad_zero.astype(jnp.bfloat16), out_weight[0].T, preferred_element_type=jnp.float32)
    attn_one = jnp.dot(grad_one.astype(jnp.bfloat16), out_weight[1].T, preferred_element_type=jnp.float32)
    attn_grads = jnp.stack([attn_zero, attn_one]).astype(jnp.bfloat16)
    input_grads = jnp.stack([input_zero, input_one])
    return (attn_grads, input_grads)
```

```python
import jax
import jax.numpy as jnp
from jax import lax
from jax.sharding import Mesh, PartitionSpec as P

D = 8192
epsilon = 1e-05
SEQ = ("z", "xh")


def body(layer_input, norm_gain, kv_cotangent, kv_weight, mlp_grads, output_cotangent, out_weight):
    section_index = lax.axis_index("section")
    h = lax.axis_index("xh")
    swap = [(0, 1), (1, 0)]
    values = layer_input[0].astype(jnp.float32)
    gain = norm_gain[0]
    squares = jnp.sum(values * values, axis=1)
    kvw = lax.all_gather(kv_weight[0], "z", axis=0)
    kvw = lax.all_to_all(kvw, "tp", 0, 0, tiled=True).reshape(2048, 512)
    out_w = lax.all_gather(out_weight[0], "z", axis=0)
    mine = kv_cotangent[0]
    theirs = lax.ppermute(mine, "xh", swap)
    cot = jnp.stack([mine, theirs])
    cot = lax.all_gather(cot, "tp", axis=2, tiled=True)
    terms_own = jnp.dot(cot[0], kvw, preferred_element_type=jnp.float32)
    terms_their = jnp.dot(cot[1], kvw, preferred_element_type=jnp.float32).astype(jnp.bfloat16)
    arrived = lax.ppermute(terms_their, "xh", swap).astype(jnp.float32)
    kv_share = jnp.where(
        h == 0,
        jnp.concatenate([terms_own, arrived], axis=1),
        jnp.concatenate([arrived, terms_own], axis=1),
    )
    squares, intersection = lax.psum((squares, jnp.sum(gain * kv_share * values, axis=1)), "tp")
    inv_rms = lax.rsqrt(squares / D + epsilon)[:, None]
    norm_back = (
        inv_rms * gain * kv_share
        - values * (inv_rms * inv_rms * inv_rms) * intersection[:, None] / D
    )
    branch = mlp_grads[0].astype(jnp.float32)
    grad_one = output_cotangent.astype(jnp.float32) + branch
    input_one = (grad_one + norm_back).astype(jnp.bfloat16)
    arriving = lax.ppermute(input_one, "section", [(1, 0)])
    grad_zero = arriving.astype(jnp.float32) + branch
    upstream = section_index == 0
    input_part = jnp.where(upstream, (grad_zero + norm_back).astype(jnp.bfloat16), input_one)
    grad_cast = jnp.where(upstream, grad_zero, grad_one).astype(jnp.bfloat16)
    left, right = grad_cast[:, :512], grad_cast[:, 512:]
    keep = jnp.where(h == 0, left, right)
    give = jnp.where(h == 0, right, left)
    got = lax.ppermute(give, "xh", swap)
    pair = lax.all_gather(jnp.stack([keep, got]), "tp", axis=0)
    parts = lax.dot_general(
        pair.transpose(1, 2, 0, 3).reshape(512, 4096),
        out_w.transpose(1, 0, 2).reshape(1024, 4096),
        (((1,), (1,)), ((), ())),
        preferred_element_type=jnp.float32,
    )
    other = lax.ppermute(parts[256:].astype(jnp.bfloat16), "xh", swap)
    attn = parts[:256] + other.astype(jnp.float32)
    return (attn.astype(jnp.bfloat16)[None], input_part[None])


def solution(mesh):
    seq = mesh.shape["seq"]
    fine = Mesh(
        mesh.devices.reshape(mesh.shape["section"], seq // 2, 2, mesh.shape["tp"]),
        ("section", "z", "xh", "tp"),
    )
    in_specs = (
        P("section", SEQ, "tp"),
        P("section", "tp"),
        P("section", SEQ, "tp"),
        P("section", "tp", SEQ),
        P("section", SEQ, "tp"),
        P(SEQ, "tp"),
        P("section", "tp", SEQ),
    )
    out_specs = (P("section", SEQ, "tp"), P("section", SEQ, "tp"))
    return jax.shard_map(body, mesh=fine, in_specs=in_specs, out_specs=out_specs, check_vma=False)
```

```python
import jax
import jax.numpy as jnp
from jax import lax
from jax.experimental import pallas as pl
from jax.experimental.pallas import tpu as pltpu
from jax.sharding import Mesh, PartitionSpec as P

D = 8192
epsilon = 1e-05
SEQ = ("z", "xh")
Z = 8
CHUNKS = 2
F32, BF16 = jnp.float32, jnp.bfloat16


def rcopy(src, dst, send_sem, recv_sem, **to):
    return pltpu.make_async_remote_copy(
        src_ref=src, dst_ref=dst, send_sem=send_sem, recv_sem=recv_sem,
        device_id=to, device_id_type=pl.DeviceIdType.MESH,
    )


def arrived(ref, sem):
    pltpu.make_async_copy(ref, ref, sem).wait()


def kernel(
    li, gain, cot_hbm, kvw_hbm, mlp, oc, wo_hbm, attn_out, ig_out,
    cotb, wz, wk, pair, wo, own_terms, their_terms, tin, give, arr, stat, coef, acc, back, pout, pin,
    kv_s, kv_r, a2a_s, a2a_r, cot_s, cot_r, gr_s, gr_r, st_s, st_r, wo_s, wo_r, one_s, one_r, loc,
):
    s, z = lax.axis_index("section"), lax.axis_index("z")
    h, t = lax.axis_index("xh"), lax.axis_index("tp")
    hp = 1 - h
    y, c = t // 2, t % 2
    zr, zl = (z + 1) % Z, (z + Z - 1) % Z
    yr, yl, yo = [((y + i) % 4) * 2 + c for i in (1, 3, 2)]
    core, yr_c, yl_c, yo_c = [i + 1 - 2 * c for i in (t, yr, yl, yo)]

    barrier = pltpu.get_barrier_semaphore()
    greet = [{"xh": hp}, {"section": 1 - s}, {"z": zr}, {"z": zl}]
    greet += [{"tp": (t + i) % Z} for i in range(1, Z)]
    for to in greet:
        pl.semaphore_signal(barrier, inc=1, device_id=to, device_id_type=pl.DeviceIdType.MESH)
    pl.semaphore_wait(barrier, len(greet))

    sent = []

    def send(src, dst, send_sem, recv_sem, **to):
        copy = rcopy(src, dst, send_sem, recv_sem, **to)
        copy.start()
        sent.append(copy)

    def ring_start(own, slot, ss, rs):
        send(own, slot(z), ss.at[0], rs.at[0], z=zr)
        send(own, slot(z), ss.at[4], rs.at[4], z=zl)

    def ring_step(k, slot, rows, ss, rs):
        a, b = (z + Z - k) % Z, (z + k) % Z
        first, last = pl.ds(0, rows // 2), pl.ds(rows // 2, rows // 2)
        if k < 4:
            arrived(slot(a), rs.at[k - 1])
            part = slot(a) if k < 3 else slot(a).at[first]
            send(part, part, ss.at[k], rs.at[k], z=zr)
            arrived(slot(b), rs.at[k + 3])
            part = slot(b) if k < 3 else slot(b).at[last]
            send(part, part, ss.at[k + 4], rs.at[k + 4], z=zl)
        else:
            arrived(slot(a).at[first], rs.at[3])
            arrived(slot(a).at[last], rs.at[7])

    def swap_start(buf, ss, rs):
        own = buf.at[t]
        send(own, own, ss.at[0], rs.at[0], tp=yr)
        send(own, own, ss.at[1], rs.at[1], tp=yl)
        send(own, own, ss.at[2], rs.at[4], tp=core)

    def swap_near(buf, ss, rs):
        arrived(buf.at[yl], rs.at[0])
        send(buf.at[yl, 0], buf.at[yl, 0], ss.at[3], rs.at[2], tp=yr)
        send(buf.at[yl], buf.at[yl], ss.at[4], rs.at[5], tp=core)
        arrived(buf.at[yr], rs.at[1])
        send(buf.at[yr, 1], buf.at[yr, 1], ss.at[5], rs.at[3], tp=yl)
        send(buf.at[yr], buf.at[yr], ss.at[6], rs.at[6], tp=core)

    def swap_far(buf, ss, rs):
        arrived(buf.at[yo, 0], rs.at[2])
        arrived(buf.at[yo, 1], rs.at[3])
        send(buf.at[yo], buf.at[yo], ss.at[7], rs.at[7], tp=core)

    def swap_end(buf, rs):
        for index, place in enumerate((core, yl_c, yr_c, yo_c)):
            arrived(buf.at[place], rs.at[4 + index])

    def pass_on(block, zz):
        @pl.when(zz == t)
        def _():
            pltpu.make_async_copy(block, wk.at[t], a2a_r.at[t]).start()

        @pl.when(zz != t)
        def _():
            rcopy(block, wk.at[t], a2a_s.at[zz], a2a_r.at[t], tp=zz).start()

    kv_slot = lambda i: wz.at[i]
    chunk_rows = 1024 // CHUNKS
    wo_slot = lambda j: (lambda i: wo.at[i, pl.ds(j * chunk_rows, chunk_rows)])

    def kv_step(k):
        ring_step(k, kv_slot, 256, kv_s, kv_r)
        if k < 4:
            pass_on(wz.at[(z + Z - k) % Z], (z + Z - k) % Z)
            pass_on(wz.at[(z + k) % Z], (z + k) % Z)
        else:
            pass_on(wz.at[(z + 4) % Z], (z + 4) % Z)

    def wo_step(k):
        for j in range(CHUNKS):
            ring_step(k, wo_slot(j), chunk_rows, wo_s.at[j], wo_r.at[j])

    ring_start(kvw_hbm, kv_slot, kv_s, kv_r)
    send(cot_hbm, cotb.at[t, h], one_s.at[0], one_r.at[0], xh=hp)
    cot_own = pltpu.make_async_copy(cot_hbm, cotb.at[t, h], loc.at[0])
    cot_own.start()
    wo_own = pltpu.make_async_copy(wo_hbm, wo.at[z], loc.at[1])
    wo_own.start()
    pass_on(kvw_hbm, z)

    @pl.loop(0, 8)
    def _(i):
        rows = pl.ds(pl.multiple_of(i * 32, 32), 32)
        v = li[rows, :].astype(F32)
        coef[rows, :] = jnp.broadcast_to(jnp.sum(v * v, axis=1, keepdims=True), (32, 128))

    cot_own.wait()
    arrived(cotb.at[t, hp], one_r.at[0])
    swap_start(cotb, cot_s, cot_r)
    kv_step(1)
    for j in range(CHUNKS):
        ring_start(wo_hbm.at[pl.ds(j * chunk_rows, chunk_rows)], wo_slot(j), wo_s.at[j], wo_r.at[j])
    swap_near(cotb, cot_s, cot_r)
    kv_step(2)
    swap_far(cotb, cot_s, cot_r)
    kv_step(3)
    kv_step(4)
    swap_end(cotb, cot_r)
    for i in range(Z):
        arrived(wk.at[i], a2a_r.at[i])

    def terms(half, into):
        into[...] = jnp.dot(cotb[0, half], wk[0], preferred_element_type=F32)

        @pl.loop(1, Z)
        def _(i):
            into[...] += jnp.dot(cotb[i, half], wk[i], preferred_element_type=F32)

    terms(hp, own_terms)
    their_terms[...] = own_terms[...].astype(BF16)
    send(their_terms, tin, one_s.at[1], one_r.at[1], xh=hp)
    terms(h, own_terms)

    mine = pl.ds(pl.multiple_of(h * 512, 512), 512)
    other = pl.ds(pl.multiple_of(hp * 512, 512), 512)
    lane = lax.broadcasted_iota(jnp.int32, (32, 128), 1)
    arrived(tin, one_r.at[1])

    @pl.loop(0, 8)
    def _(i):
        rows = pl.ds(pl.multiple_of(i * 32, 32), 32)
        inner = jnp.sum(gain[:, mine] * own_terms[rows, :] * li[rows, mine].astype(F32), axis=1, keepdims=True)
        inner += jnp.sum(
            gain[:, other] * tin[rows, :].astype(F32) * li[rows, other].astype(F32), axis=1, keepdims=True
        )
        coef[rows, :] = jnp.where(lane == 0, coef[rows, :], jnp.broadcast_to(inner, (32, 128)))

    stat[t] = coef[...].T[:8]
    for i in range(1, Z):
        send(stat.at[t], stat.at[t], st_s.at[i], st_r.at[t], tp=(t + i) % Z)
    for i in range(1, Z):
        place = (t + i) % Z
        arrived(stat.at[place], st_r.at[place])
    total = stat[0]
    for i in range(1, Z):
        total += stat[i]
    inv = lax.rsqrt(total / D + epsilon)
    inv = jnp.broadcast_to(inv[0:1], (8, 256))
    both = jnp.where(
        lax.broadcasted_iota(jnp.int32, (8, 256), 0) == 0, inv, inv * inv * inv * total / D
    )
    coef[...] = jnp.concatenate([both] * 16, axis=0).T

    @pl.loop(0, 8)
    def _(i):
        rows = pl.ds(pl.multiple_of(i * 32, 32), 32)
        scale, shift = coef[rows, 0:1], coef[rows, 1:2]
        back[rows, mine] = scale * gain[:, mine] * own_terms[rows, :] - li[rows, mine].astype(F32) * shift
        back[rows, other] = (
            scale * gain[:, other] * tin[rows, :].astype(F32) - li[rows, other].astype(F32) * shift
        )

    onward = rcopy(ig_out, arr, one_s.at[2], one_r.at[2], section=1 - s)

    @pl.when(s == 1)
    def _():
        @pl.loop(0, 8)
        def _(i):
            rows = pl.ds(pl.multiple_of(i * 32, 32), 32)
            grad = oc[rows, :].astype(F32) + mlp[rows, :].astype(F32)
            ig_out[rows, :] = (grad + back[rows, :]).astype(BF16)

        onward.start()

    wo_step(1)

    def cast(first):
        @pl.loop(0, 8)
        def _(i):
            rows = pl.ds(pl.multiple_of(i * 32, 32), 32)
            pair[t, h, rows, :] = (first[rows, mine].astype(F32) + mlp[rows, mine].astype(F32)).astype(BF16)
            give[rows, :] = (first[rows, other].astype(F32) + mlp[rows, other].astype(F32)).astype(BF16)

    @pl.when(s == 1)
    def _():
        cast(oc)

    @pl.when(s == 0)
    def _():
        arrived(arr, one_r.at[2])
        cast(arr)

    send(give, pair.at[t, h], one_s.at[3], one_r.at[3], xh=hp)

    @pl.when(s == 0)
    def _():
        @pl.loop(0, 8)
        def _(i):
            rows = pl.ds(pl.multiple_of(i * 32, 32), 32)
            grad = arr[rows, :].astype(F32) + mlp[rows, :].astype(F32)
            ig_out[rows, :] = (grad + back[rows, :]).astype(BF16)

    arrived(pair.at[t, hp], one_r.at[3])
    swap_start(pair, gr_s, gr_r)
    wo_step(2)
    swap_near(pair, gr_s, gr_r)
    swap_far(pair, gr_s, gr_r)
    wo_step(3)
    swap_end(pair, gr_r)
    wo_own.wait()

    def block(i, first=False):
        @pl.loop(0, 4)
        def _(n):
            columns = pl.ds(pl.multiple_of(n * 256, 256), 256)
            product = lax.dot_general(
                pair[i].reshape(512, 512), wo[i, columns, :],
                (((1,), (1,)), ((), ())), preferred_element_type=F32,
            )
            if first:
                acc[:, columns] = product
            else:
                acc[:, columns] += product

    block(z, True)
    for k in (1, 2, 3):
        block((z + Z - k) % Z)
        block((z + k) % Z)
    wo_step(4)
    block((z + 4) % Z)
    theirs = pl.ds(pl.multiple_of(hp * 256, 256), 256)
    ours = pl.ds(pl.multiple_of(h * 256, 256), 256)
    pout[...] = acc[theirs, :].astype(BF16)
    send(pout, pin, one_s.at[4], one_r.at[4], xh=hp)
    arrived(pin, one_r.at[4])
    attn_out[...] = (acc[ours, :] + pin[...].astype(F32)).astype(BF16)

    for copy in sent:
        copy.wait_send()
    for i in range(Z):
        @pl.when(i != t)
        def _():
            rcopy(wk.at[t], wk.at[t], a2a_s.at[i], a2a_r.at[t], tp=i).wait_send()

    @pl.when(s == 1)
    def _():
        onward.wait_send()


def body(layer_input, norm_gain, kv_cotangent, kv_weight, mlp_grads, output_cotangent, out_weight):
    vmem, hbm = pl.BlockSpec(memory_space=pltpu.VMEM), pl.BlockSpec(memory_space=pl.ANY)
    dma = lambda *n: pltpu.SemaphoreType.DMA(n)
    out = jax.ShapeDtypeStruct((256, 1024), BF16)
    attn, grads = pl.pallas_call(
        kernel,
        out_shape=(out, out),
        in_specs=[vmem, vmem, hbm, hbm, vmem, vmem, hbm],
        out_specs=(vmem, vmem),
        scratch_shapes=[
            pltpu.VMEM((Z, 2, 256, 256), BF16),
            pltpu.VMEM((Z, 256, 512), BF16),
            pltpu.VMEM((Z, 256, 512), BF16),
            pltpu.VMEM((Z, 2, 256, 512), BF16),
            pltpu.VMEM((Z, 1024, 512), BF16),
            pltpu.VMEM((256, 512), F32),
            pltpu.VMEM((256, 512), BF16),
            pltpu.VMEM((256, 512), BF16),
            pltpu.VMEM((256, 512), BF16),
            pltpu.VMEM((256, 1024), BF16),
            pltpu.VMEM((Z, 8, 256), F32),
            pltpu.VMEM((256, 128), F32),
            pltpu.VMEM((512, 1024), F32),
            pltpu.VMEM((256, 1024), F32),
            pltpu.VMEM((256, 1024), BF16),
            pltpu.VMEM((256, 1024), BF16),
            dma(8), dma(8),
            dma(8), dma(8),
            dma(8), dma(8),
            dma(8), dma(8),
            dma(8), dma(8),
            dma(CHUNKS, 8), dma(CHUNKS, 8),
            dma(5), dma(5),
            dma(2),
        ],
        compiler_params=pltpu.CompilerParams(
            collective_id=0, has_side_effects=True, vmem_limit_bytes=48 * 2**20
        ),
    )(
        layer_input[0], norm_gain, kv_cotangent[0], kv_weight[0],
        mlp_grads[0], output_cotangent, out_weight[0],
    )
    return attn[None], grads[None]


def solution(mesh):
    fine = Mesh(
        mesh.devices.reshape(mesh.shape["section"], Z, 2, mesh.shape["tp"]),
        ("section", "z", "xh", "tp"),
    )
    in_specs = (
        P("section", SEQ, "tp"),
        P("section", "tp"),
        P("section", SEQ, "tp"),
        P("section", "tp", SEQ),
        P("section", SEQ, "tp"),
        P(SEQ, "tp"),
        P("section", "tp", SEQ),
    )
    out_specs = (P("section", SEQ, "tp"), P("section", SEQ, "tp"))
    return jax.shard_map(body, mesh=fine, in_specs=in_specs, out_specs=out_specs, check_vma=False)
```

```python
import jax
import jax.numpy as jnp
from jax import lax
from jax.experimental import pallas as pl
from jax.experimental.pallas import tpu as pltpu
from jax.sharding import Mesh, PartitionSpec as P

D = 8192
epsilon = 1e-05
SEQ = ("z", "xh")
Z = 8
CHUNKS = 4
KV_CHUNKS = 4
F32, BF16 = jnp.float32, jnp.bfloat16


def rcopy(src, dst, send_sem, recv_sem, **to):
    return pltpu.make_async_remote_copy(
        src_ref=src, dst_ref=dst, send_sem=send_sem, recv_sem=recv_sem,
        device_id=to, device_id_type=pl.DeviceIdType.MESH,
    )


def arrived(ref, sem):
    pltpu.make_async_copy(ref, ref, sem).wait()


def kernel(
    li_hbm, gain_hbm, cot_hbm, kvw_hbm, mlp_hbm, oc_hbm, wo_hbm, attn_out, ig_out,
    li, gain, mlp, oc, cotb, wz, wk, pair, wo, own_terms, their_terms, tin, give,
    far_in, keep_in, rest_in, stat, coef, acc, pout, pin,
    kv_s, kv_r, a2a_s, a2a_r, cot_s, cot_r, gr_s, gr_r, st_s, st_r, wo_s, wo_r, one_s, one_r, out_s, out_r, loc,
):
    s, z = lax.axis_index("section"), lax.axis_index("z")
    h, t = lax.axis_index("xh"), lax.axis_index("tp")
    hp = 1 - h
    y, c = t // 2, t % 2
    zr, zl = (z + 1) % Z, (z + Z - 1) % Z
    yr, yl, yo = [((y + i) % 4) * 2 + c for i in (1, 3, 2)]
    core, yr_c, yl_c, yo_c = [i + 1 - 2 * c for i in (t, yr, yl, yo)]
    mine = pl.ds(pl.multiple_of(h * 512, 512), 512)
    other = pl.ds(pl.multiple_of(hp * 512, 512), 512)

    loads = [
        pltpu.make_async_copy(src, dst, loc.at[i])
        for i, (src, dst) in enumerate(((li_hbm, li), (gain_hbm, gain), (mlp_hbm, mlp), (oc_hbm, oc)))
    ]
    cot_own = pltpu.make_async_copy(cot_hbm, cotb.at[t, h], loc.at[4])
    wo_own = pltpu.make_async_copy(wo_hbm, wo.at[z], loc.at[5])
    for load in [cot_own] + loads + [wo_own]:
        load.start()

    barrier = pltpu.get_barrier_semaphore()
    greet = [{"xh": hp}, {"section": 1 - s}, {"section": 1 - s, "xh": hp}, {"z": zr}, {"z": zl}]
    greet += [{"tp": (t + i) % Z} for i in range(1, Z)]
    for to in greet:
        pl.semaphore_signal(barrier, inc=1, device_id=to, device_id_type=pl.DeviceIdType.MESH)
    pl.semaphore_wait(barrier, len(greet))

    sent = []

    def send(src, dst, send_sem, recv_sem, **to):
        copy = rcopy(src, dst, send_sem, recv_sem, **to)
        copy.start()
        sent.append(copy.wait_send)

    def finish():
        for wait in sent:
            wait()

    def ring_start(own, slot, ss, rs):
        send(own, slot(z), ss.at[0], rs.at[0], z=zr)
        send(own, slot(z), ss.at[4], rs.at[4], z=zl)

    def ring_step(k, slot, rows, ss, rs):
        a, b = (z + Z - k) % Z, (z + k) % Z
        first, last = pl.ds(0, rows // 2), pl.ds(rows // 2, rows // 2)
        if k < 4:
            arrived(slot(a), rs.at[k - 1])
            part = slot(a) if k < 3 else slot(a).at[first]
            send(part, part, ss.at[k], rs.at[k], z=zr)
            arrived(slot(b), rs.at[k + 3])
            part = slot(b) if k < 3 else slot(b).at[last]
            send(part, part, ss.at[k + 4], rs.at[k + 4], z=zl)
        else:
            arrived(slot(a).at[first], rs.at[3])
            arrived(slot(a).at[last], rs.at[7])

    def swap_start(whole, ss, rs):
        own = whole(t)
        send(own, own, ss.at[0], rs.at[0], tp=yr)
        send(own, own, ss.at[1], rs.at[1], tp=yl)
        send(own, own, ss.at[2], rs.at[4], tp=core)

    def swap_near(whole, lower, upper, ss, rs):
        arrived(whole(yl), rs.at[0])
        send(lower(yl), lower(yl), ss.at[3], rs.at[2], tp=yr)
        send(whole(yl), whole(yl), ss.at[4], rs.at[5], tp=core)
        arrived(whole(yr), rs.at[1])
        send(upper(yr), upper(yr), ss.at[5], rs.at[3], tp=yl)
        send(whole(yr), whole(yr), ss.at[6], rs.at[6], tp=core)

    def swap_far(whole, lower, upper, ss, rs):
        arrived(lower(yo), rs.at[2])
        arrived(upper(yo), rs.at[3])
        send(whole(yo), whole(yo), ss.at[7], rs.at[7], tp=core)

    def swap_end(whole, rs):
        for index, place in enumerate((core, yl_c, yr_c, yo_c)):
            arrived(whole(place), rs.at[4 + index])

    kv_rows = 256 // KV_CHUNKS
    kv_part = [pl.ds(j * kv_rows, kv_rows) for j in range(KV_CHUNKS)]

    def kv_start(j):
        ring_start(kvw_hbm.at[kv_part[j]], lambda i: wz.at[i, kv_part[j]], kv_s.at[j], kv_r.at[j])

    def kv_step(k, j):
        ring_step(k, lambda i: wz.at[i, kv_part[j]], kv_rows, kv_s.at[j], kv_r.at[j])

    def pass_on(j):
        land = wk.at[t, kv_part[j]]
        for i in range(1, Z):
            zz = (t + i) % Z
            pl.when(zz != z)(
                rcopy(wz.at[zz, kv_part[j]], land, a2a_s.at[j, i], a2a_r.at[j, t], tp=zz).start
            )
            pl.when(zz == z)(
                rcopy(kvw_hbm.at[kv_part[j]], land, a2a_s.at[j, i], a2a_r.at[j, t], tp=zz).start
            )
            sent.append(rcopy(wz.at[zz, kv_part[j]], land, a2a_s.at[j, i], a2a_r.at[j, t], tp=zz).wait_send)
        pl.when(t != z)(pltpu.make_async_copy(wz.at[t, kv_part[j]], land, a2a_r.at[j, t]).start)
        pl.when(t == z)(pltpu.make_async_copy(kvw_hbm.at[kv_part[j]], land, a2a_r.at[j, t]).start)

    wo_rows = 1024 // CHUNKS
    wo_part = [pl.ds(j * wo_rows, wo_rows) for j in range(CHUNKS)]

    def wo_step(k, j):
        ring_step(k, lambda i: wo.at[i, wo_part[j]], wo_rows, wo_s.at[j], wo_r.at[j])

    cot_whole, cot_lower, cot_upper = lambda i: cotb.at[i], lambda i: cotb.at[i, 0], lambda i: cotb.at[i, 1]

    half_kv = KV_CHUNKS // 2
    group_a, group_b = range(half_kv), range(half_kv, KV_CHUNKS)
    for j in group_a:
        kv_start(j)
    send(cot_hbm, cotb.at[t, h], one_s.at[0], one_r.at[0], xh=hp)
    for load in loads:
        load.wait()

    @pl.when(s == 1)
    def _():
        @pl.loop(0, 8)
        def _(i):
            rows = pl.ds(pl.multiple_of(i * 32, 32), 32)
            pair[t, h, rows, :] = (oc[rows, mine].astype(F32) + mlp[rows, mine].astype(F32)).astype(BF16)
            give[rows, :] = (oc[rows, other].astype(F32) + mlp[rows, other].astype(F32)).astype(BF16)

    @pl.when(s == 0)
    def _():
        give[...] = mlp[:, other]

    send(give, pair.at[t, h], one_s.at[3], one_r.at[3], xh=hp)
    cot_own.wait()
    arrived(cotb.at[t, hp], one_r.at[0])
    swap_start(cot_whole, cot_s, cot_r)
    for k in (1, 2):
        for j in group_a:
            kv_step(k, j)
    for j in group_b:
        kv_start(j)
    for j in group_a:
        kv_step(3, j)

    @pl.loop(0, 8)
    def _(i):
        rows = pl.ds(pl.multiple_of(i * 32, 32), 32)
        v = li[rows, :].astype(F32)
        coef[rows, :] = jnp.broadcast_to(jnp.sum(v * v, axis=1, keepdims=True), (32, 128))

    swap_near(cot_whole, cot_lower, cot_upper, cot_s, cot_r)
    for j in group_a:
        kv_step(4, j)
        pass_on(j)
    for j in group_b:
        kv_step(1, j)
    swap_far(cot_whole, cot_lower, cot_upper, cot_s, cot_r)
    for k in (2, 3):
        for j in group_b:
            kv_step(k, j)
    for j in range(CHUNKS):
        ring_start(wo_hbm.at[wo_part[j]], lambda i: wo.at[i, wo_part[j]], wo_s.at[j], wo_r.at[j])
    for j in group_b:
        kv_step(4, j)
        pass_on(j)
    swap_end(cot_whole, cot_r)
    for j in range(KV_CHUNKS):
        for i in range(Z):
            arrived(wk.at[i, kv_part[j]], a2a_r.at[j, i])

    def terms(half, into):
        into[...] = jnp.dot(cotb[0, half], wk[0], preferred_element_type=F32)

        @pl.loop(1, Z)
        def _(i):
            into[...] += jnp.dot(cotb[i, half], wk[i], preferred_element_type=F32)

    terms(hp, own_terms)
    their_terms[...] = own_terms[...].astype(BF16)
    send(their_terms, tin, one_s.at[1], one_r.at[1], xh=hp)
    wo_step(1, 0)
    terms(h, own_terms)
    lane = lax.broadcasted_iota(jnp.int32, (32, 128), 1)
    wo_step(1, 1)
    arrived(tin, one_r.at[1])

    @pl.loop(0, 8)
    def _(i):
        rows = pl.ds(pl.multiple_of(i * 32, 32), 32)
        inner = jnp.sum(gain[:, mine] * own_terms[rows, :] * li[rows, mine].astype(F32), axis=1, keepdims=True)
        inner += jnp.sum(
            gain[:, other] * tin[rows, :].astype(F32) * li[rows, other].astype(F32), axis=1, keepdims=True
        )
        coef[rows, :] = jnp.where(lane == 0, coef[rows, :], jnp.broadcast_to(inner, (32, 128)))

    stat[t] = coef[...].T[:8]
    for i in range(1, Z):
        send(stat.at[t], stat.at[t], st_s.at[i], st_r.at[t], tp=(t + i) % Z)
    wo_step(1, 2)
    for i in range(1, Z):
        place = (t + i) % Z
        arrived(stat.at[place], st_r.at[place])
    total = stat[0]
    for i in range(1, Z):
        total += stat[i]
    inv = lax.rsqrt(total / D + epsilon)
    inv = jnp.broadcast_to(inv[0:1], (8, 256))
    both = jnp.where(
        lax.broadcasted_iota(jnp.int32, (8, 256), 0) == 0, inv, inv * inv * inv * total / D
    )
    coef[...] = jnp.concatenate([both] * 16, axis=0).T

    def norm_back(rows, columns, terms_ref):
        return (
            coef[rows, 0:1] * gain[:, columns] * terms_ref[rows, :].astype(F32)
            - li[rows, columns].astype(F32) * coef[rows, 1:2]
        )

    to_far = rcopy(ig_out.at[:, other], far_in, one_s.at[2], one_r.at[2], section=1 - s, xh=hp)
    to_keep = rcopy(ig_out.at[:, mine], keep_in, one_s.at[4], one_r.at[4], section=1 - s)
    to_rest = rcopy(ig_out.at[:, other], rest_in, one_s.at[5], one_r.at[5], section=1 - s)
    for copy in (to_far, to_keep, to_rest):
        sent.append(lambda copy=copy: pl.when(s == 1)(copy.wait_send))

    @pl.when(s == 1)
    def _():
        def down(columns, terms_ref):
            @pl.loop(0, 8)
            def _(i):
                rows = pl.ds(pl.multiple_of(i * 32, 32), 32)
                grad = oc[rows, columns].astype(F32) + mlp[rows, columns].astype(F32)
                ig_out[rows, columns] = (grad + norm_back(rows, columns, terms_ref)).astype(BF16)

        down(other, tin)
        to_far.start()
        down(mine, own_terms)
        to_keep.start()
        to_rest.start()

    wo_step(1, 3)
    arrived(pair.at[t, hp], one_r.at[3])

    def pair_refs(half):
        return (
            lambda i: pair.at[i, half], lambda i: pair.at[i, half, pl.ds(0, 128)],
            lambda i: pair.at[i, half, pl.ds(128, 128)],
        )

    theirs, ours = pair_refs(hp), pair_refs(h)

    @pl.when(s == 0)
    def _():
        arrived(far_in, one_r.at[2])

        @pl.loop(0, 8)
        def _(i):
            rows = pl.ds(pl.multiple_of(i * 32, 32), 32)
            pair[t, hp, rows, :] = (far_in[rows, :].astype(F32) + pair[t, hp, rows, :].astype(F32)).astype(BF16)

    swap_start(theirs[0], gr_s.at[0], gr_r.at[0])

    @pl.when(s == 0)
    def _():
        arrived(keep_in, one_r.at[4])

        @pl.loop(0, 8)
        def _(i):
            rows = pl.ds(pl.multiple_of(i * 32, 32), 32)
            pair[t, h, rows, :] = (keep_in[rows, :].astype(F32) + mlp[rows, mine].astype(F32)).astype(BF16)

    swap_start(ours[0], gr_s.at[1], gr_r.at[1])

    wo_step(2, 0)
    wo_step(2, 1)
    swap_near(*theirs, gr_s.at[0], gr_r.at[0])
    wo_step(2, 2)

    @pl.when(s == 0)
    def _():
        arrived(rest_in, one_r.at[5])

        def up(columns, terms_ref, from_ref):
            @pl.loop(0, 8)
            def _(i):
                rows = pl.ds(pl.multiple_of(i * 32, 32), 32)
                grad = from_ref[rows, :].astype(F32) + mlp[rows, columns].astype(F32)
                ig_out[rows, columns] = (grad + norm_back(rows, columns, terms_ref)).astype(BF16)

        up(mine, own_terms, keep_in)
        up(other, tin, rest_in)

    swap_near(*ours, gr_s.at[1], gr_r.at[1])
    swap_far(*theirs, gr_s.at[0], gr_r.at[0])
    wo_step(2, 3)
    swap_far(*ours, gr_s.at[1], gr_r.at[1])
    swap_end(theirs[0], gr_r.at[0])
    wo_own.wait()
    wo_step(3, 0)

    def product(half, i, columns):
        return lax.dot_general(
            pair[i, half], wo[i, columns, :], (((1,), (1,)), ((), ())), preferred_element_type=F32
        )

    near = [z] + [(z + k) % Z for k in (Z - 1, 1, Z - 2, 2)]

    def first_blocks(half):
        @pl.loop(0, 4)
        def _(n):
            columns = pl.ds(pl.multiple_of(n * 256, 256), 256)
            total = product(half, near[0], columns)
            for i in near[1:]:
                total += product(half, i, columns)
            acc[half, :, columns] = total

    first_blocks(hp)
    wo_step(3, 1)
    swap_end(ours[0], gr_r.at[1])
    first_blocks(h)
    for j in range(CHUNKS):
        if j > 1:
            wo_step(3, j)
        for half in (hp, h):
            acc[half, :, wo_part[j]] += product(half, (z + 3) % Z, wo_part[j]) + product(
                half, (z + Z - 3) % Z, wo_part[j]
            )
    for j in range(CHUNKS):
        wo_step(4, j)
        far = (z + 4) % Z
        pout[j] = (acc[hp, :, wo_part[j]] + product(hp, far, wo_part[j])).astype(BF16)
        send(pout.at[j], pin.at[j], out_s.at[j], out_r.at[j], xh=hp)
        acc[h, :, wo_part[j]] += product(h, far, wo_part[j])
    for j in range(CHUNKS):
        arrived(pin.at[j], out_r.at[j])
        attn_out[:, wo_part[j]] = (acc[h, :, wo_part[j]] + pin[j].astype(F32)).astype(BF16)
    finish()


def body(layer_input, norm_gain, kv_cotangent, kv_weight, mlp_grads, output_cotangent, out_weight):
    vmem, hbm = pl.BlockSpec(memory_space=pltpu.VMEM), pl.BlockSpec(memory_space=pltpu.HBM)
    dma = lambda *n: pltpu.SemaphoreType.DMA(n)
    out = jax.ShapeDtypeStruct((256, 1024), BF16)
    attn, grads = pl.pallas_call(
        kernel,
        out_shape=(out, out),
        in_specs=[hbm] * 7,
        out_specs=(vmem, vmem),
        scratch_shapes=[
            pltpu.VMEM((256, 1024), BF16),
            pltpu.VMEM((1, 1024), F32),
            pltpu.VMEM((256, 1024), BF16),
            pltpu.VMEM((256, 1024), BF16),
            pltpu.VMEM((Z, 2, 256, 256), BF16),
            pltpu.VMEM((Z, 256, 512), BF16),
            pltpu.VMEM((Z, 256, 512), BF16),
            pltpu.VMEM((Z, 2, 256, 512), BF16),
            pltpu.VMEM((Z, 1024, 512), BF16),
            pltpu.VMEM((256, 512), F32),
            pltpu.VMEM((256, 512), BF16),
            pltpu.VMEM((256, 512), BF16),
            pltpu.VMEM((256, 512), BF16),
            pltpu.VMEM((256, 512), BF16),
            pltpu.VMEM((256, 512), BF16),
            pltpu.VMEM((256, 512), BF16),
            pltpu.VMEM((Z, 8, 256), F32),
            pltpu.VMEM((256, 128), F32),
            pltpu.VMEM((2, 256, 1024), F32),
            pltpu.VMEM((CHUNKS, 256, 1024 // CHUNKS), BF16),
            pltpu.VMEM((CHUNKS, 256, 1024 // CHUNKS), BF16),
            dma(KV_CHUNKS, 8), dma(KV_CHUNKS, 8),
            dma(KV_CHUNKS, 8), dma(KV_CHUNKS, 8),
            dma(8), dma(8),
            dma(2, 8), dma(2, 8),
            dma(8), dma(8),
            dma(CHUNKS, 8), dma(CHUNKS, 8),
            dma(6), dma(6),
            dma(CHUNKS), dma(CHUNKS),
            dma(6),
        ],
        compiler_params=pltpu.CompilerParams(
            collective_id=0, has_side_effects=True, vmem_limit_bytes=58 * 2**20
        ),
    )(
        layer_input[0], norm_gain, kv_cotangent[0], kv_weight[0],
        mlp_grads[0], output_cotangent, out_weight[0],
    )
    return attn[None], grads[None]


def solution(mesh):
    fine = Mesh(
        mesh.devices.reshape(mesh.shape["section"], Z, 2, mesh.shape["tp"]),
        ("section", "z", "xh", "tp"),
    )
    in_specs = (
        P("section", SEQ, "tp"),
        P("section", "tp"),
        P("section", SEQ, "tp"),
        P("section", "tp", SEQ),
        P("section", SEQ, "tp"),
        P(SEQ, "tp"),
        P("section", "tp", SEQ),
    )
    out_specs = (P("section", SEQ, "tp"), P("section", SEQ, "tp"))
    return jax.shard_map(body, mesh=fine, in_specs=in_specs, out_specs=out_specs, check_vma=False)
```

```python
import jax
import jax.numpy as jnp
from jax import lax
from jax.experimental import pallas as pl
from jax.experimental.pallas import tpu as pltpu
from jax.sharding import Mesh, PartitionSpec as P

D = 8192
epsilon = 1e-05
SEQ = ("z", "xh")
Z = 8
CHUNKS = 8
KV_CHUNKS = 4
F32, BF16 = jnp.float32, jnp.bfloat16


def rcopy(src, dst, send_sem, recv_sem, **to):
    return pltpu.make_async_remote_copy(
        src_ref=src, dst_ref=dst, send_sem=send_sem, recv_sem=recv_sem,
        device_id=to, device_id_type=pl.DeviceIdType.MESH,
    )


def arrived(ref, sem):
    pltpu.make_async_copy(ref, ref, sem).wait()


def kernel(
    li_hbm, gain_hbm, cot_hbm, kvw_hbm, mlp_hbm, oc_hbm, wo_hbm, attn_out, ig_hbm,
    attn, ig_out,    li, gain, mlp, oc, cotb, wz, wk, pair, wo, own_terms, their_terms, tin, give,
    far_in, keep_in, rest_in, stat, coef, acc, pout, pin,
    kv_s, kv_r, a2a_s, a2a_r, cot_s, cot_r, gr_s, gr_r, st_s, st_r, wo_s, wo_r, one_s, one_r, out_s, out_r, loc, res,
):
    s, z = lax.axis_index("section"), lax.axis_index("z")
    h, t = lax.axis_index("xh"), lax.axis_index("tp")
    hp = 1 - h
    y, c = t // 2, t % 2
    zr, zl, far = (z + 1) % Z, (z + Z - 1) % Z, (z + 4) % Z
    yr, yl, yo = [((y + i) % 4) * 2 + c for i in (1, 3, 2)]
    core, yr_c, yl_c, yo_c = [i + 1 - 2 * c for i in (t, yr, yl, yo)]
    mine = pl.ds(pl.multiple_of(h * 512, 512), 512)
    other = pl.ds(pl.multiple_of(hp * 512, 512), 512)

    loads = [
        pltpu.make_async_copy(src, dst, loc.at[i])
        for i, (src, dst) in enumerate(((li_hbm, li), (gain_hbm, gain), (mlp_hbm, mlp), (oc_hbm, oc)))
    ]
    cot_own = pltpu.make_async_copy(cot_hbm, cotb.at[t, h], loc.at[4])
    wo_own = pltpu.make_async_copy(wo_hbm, wo.at[z], loc.at[5])
    kv_own = pltpu.make_async_copy(kvw_hbm, wz.at[z], loc.at[6])
    for load in [cot_own, kv_own] + loads + [wo_own]:
        load.start()

    barrier = pltpu.get_barrier_semaphore()
    greet = [{"xh": hp}, {"section": 1 - s}, {"section": 1 - s, "xh": hp}, {"z": zr}, {"z": zl}]
    greet += [{"tp": (t + i) % Z} for i in range(1, Z)]
    for to in greet:
        pl.semaphore_signal(barrier, inc=1, device_id=to, device_id_type=pl.DeviceIdType.MESH)
    pl.semaphore_wait(barrier, len(greet))

    sent = []

    def send(src, dst, send_sem, recv_sem, **to):
        copy = rcopy(src, dst, send_sem, recv_sem, **to)
        copy.start()
        sent.append(copy.wait_send)

    def finish():
        for wait in sent:
            wait()

    def ring_start(own, slot, ss, rs):
        send(own, slot(z), ss.at[0], rs.at[0], z=zr)
        send(own, slot(z), ss.at[4], rs.at[4], z=zl)

    def ring_step(k, slot, rows, ss, rs):
        a, b = (z + Z - k) % Z, (z + k) % Z
        first, last = pl.ds(0, rows // 2), pl.ds(rows // 2, rows // 2)
        if k < 4:
            arrived(slot(a), rs.at[k - 1])
            part = slot(a) if k < 3 else slot(a).at[first]
            send(part, part, ss.at[k], rs.at[k], z=zr)
            arrived(slot(b), rs.at[k + 3])
            part = slot(b) if k < 3 else slot(b).at[last]
            send(part, part, ss.at[k + 4], rs.at[k + 4], z=zl)
        else:
            arrived(slot(a).at[first], rs.at[3])
            arrived(slot(a).at[last], rs.at[7])

    def swap_start(whole, ss, rs):
        own = whole(t)
        send(own, own, ss.at[0], rs.at[0], tp=yr)
        send(own, own, ss.at[1], rs.at[1], tp=yl)
        send(own, own, ss.at[2], rs.at[4], tp=core)

    def swap_near(whole, lower, upper, ss, rs):
        arrived(whole(yl), rs.at[0])
        send(lower(yl), lower(yl), ss.at[3], rs.at[2], tp=yr)
        send(whole(yl), whole(yl), ss.at[4], rs.at[5], tp=core)
        arrived(whole(yr), rs.at[1])
        send(upper(yr), upper(yr), ss.at[5], rs.at[3], tp=yl)
        send(whole(yr), whole(yr), ss.at[6], rs.at[6], tp=core)

    def swap_far(whole, lower, upper, ss, rs):
        arrived(lower(yo), rs.at[2])
        arrived(upper(yo), rs.at[3])
        send(whole(yo), whole(yo), ss.at[7], rs.at[7], tp=core)

    def swap_end(whole, rs):
        for index, place in enumerate((core, yl_c, yr_c, yo_c)):
            arrived(whole(place), rs.at[4 + index])

    kv_rows = 256 // KV_CHUNKS
    kv_part = [pl.ds(j * kv_rows, kv_rows) for j in range(KV_CHUNKS)]

    def kv_start(j):
        own = kvw_hbm.at[kv_part[j]]
        ring_start(own, lambda i: wz.at[i, kv_part[j]], kv_s.at[j], kv_r.at[j])

    def kv_step(k, j):
        ring_step(k, lambda i: wz.at[i, kv_part[j]], kv_rows, kv_s.at[j], kv_r.at[j])

    def pass_on(j):
        land = wk.at[t, kv_part[j]]
        for i in range(1, Z):
            zz = (t + i) % Z
            send(wz.at[zz, kv_part[j]], land, a2a_s.at[j, i], a2a_r.at[j, t], tp=zz)
        pltpu.make_async_copy(wz.at[t, kv_part[j]], land, a2a_r.at[j, t]).start()

    def kv_arrived(j, i):
        arrived(wk.at[i, kv_part[j]], a2a_r.at[j, i])

    wo_rows = 1024 // CHUNKS
    wo_part = [pl.ds(j * wo_rows, wo_rows) for j in range(CHUNKS)]

    def wo_start(j):
        ring_start(wo_hbm.at[wo_part[j]], lambda i: wo.at[i, wo_part[j]], wo_s.at[j], wo_r.at[j])

    def wo_piece(k, j):
        ring_step(k, lambda i: wo.at[i, wo_part[j]], wo_rows, wo_s.at[j], wo_r.at[j])

    def wo_step(k, quarter):
        for j in range(quarter * CHUNKS // 4, (quarter + 1) * CHUNKS // 4):
            wo_piece(k, j)

    cot_whole, cot_lower, cot_upper = lambda i: cotb.at[i], lambda i: cotb.at[i, 0], lambda i: cotb.at[i, 1]

    kv_start(0)
    kv_start(1)
    cot_own.wait()
    send(cot_hbm, cotb.at[t, h], one_s.at[0], one_r.at[0], xh=hp)
    for load in loads:
        load.wait()

    @pl.when(s == 1)
    def _():
        @pl.loop(0, 8)
        def _(i):
            rows = pl.ds(pl.multiple_of(i * 32, 32), 32)
            give[rows, :] = (oc[rows, other].astype(F32) + mlp[rows, other].astype(F32)).astype(BF16)

    @pl.when(s == 0)
    def _():
        give[...] = mlp[:, other]

    send(give, pair.at[t, h], one_s.at[3], one_r.at[3], xh=hp)
    kv_step(1, 0)
    kv_step(1, 1)
    kv_start(2)
    arrived(cotb.at[t, hp], one_r.at[0])
    swap_start(cot_whole, cot_s, cot_r)
    kv_step(2, 0)
    kv_step(2, 1)
    kv_step(1, 2)
    kv_step(3, 0)
    kv_step(3, 1)
    kv_start(3)
    swap_near(cot_whole, cot_lower, cot_upper, cot_s, cot_r)
    kv_step(2, 2)
    kv_own.wait()
    kv_step(4, 0)
    pass_on(0)
    kv_step(4, 1)
    pass_on(1)
    kv_step(1, 3)
    wo_start(0)
    kv_step(3, 2)
    swap_far(cot_whole, cot_lower, cot_upper, cot_s, cot_r)
    kv_step(2, 3)
    wo_start(1)
    kv_step(4, 2)
    pass_on(2)
    kv_step(3, 3)
    for j in range(2, CHUNKS):
        wo_start(j)
    kv_step(4, 3)
    pass_on(3)

    @pl.when(s == 1)
    def _():
        @pl.loop(0, 8)
        def _(i):
            rows = pl.ds(pl.multiple_of(i * 32, 32), 32)
            pair[t, h, rows, :] = (oc[rows, mine].astype(F32) + mlp[rows, mine].astype(F32)).astype(BF16)

    @pl.loop(0, 8)
    def _(i):
        rows = pl.ds(pl.multiple_of(i * 32, 32), 32)
        v = li[rows, :].astype(F32)
        coef[rows, :] = jnp.broadcast_to(jnp.sum(v * v, axis=1, keepdims=True), (32, 128))

    swap_end(cot_whole, cot_r)
    for j in range(KV_CHUNKS):
        for i in range(Z):
            kv_arrived(j, i)

    def terms(half, into):
        into[...] = jnp.dot(cotb[0, half], wk[0], preferred_element_type=F32)

        @pl.loop(1, Z)
        def _(i):
            into[...] += jnp.dot(cotb[i, half], wk[i], preferred_element_type=F32)

    terms(hp, own_terms)
    their_terms[...] = own_terms[...].astype(BF16)
    send(their_terms, tin, one_s.at[1], one_r.at[1], xh=hp)
    wo_step(1, 0)
    terms(h, own_terms)
    lane = lax.broadcasted_iota(jnp.int32, (32, 128), 1)
    wo_step(1, 1)
    arrived(tin, one_r.at[1])

    @pl.loop(0, 8)
    def _(i):
        rows = pl.ds(pl.multiple_of(i * 32, 32), 32)
        inner = jnp.sum(gain[:, mine] * own_terms[rows, :] * li[rows, mine].astype(F32), axis=1, keepdims=True)
        inner += jnp.sum(
            gain[:, other] * tin[rows, :].astype(F32) * li[rows, other].astype(F32), axis=1, keepdims=True
        )
        coef[rows, :] = jnp.where(lane == 0, coef[rows, :], jnp.broadcast_to(inner, (32, 128)))

    stat[t] = coef[...].T[:8]
    for i in range(1, Z):
        send(stat.at[t], stat.at[t], st_s.at[i], st_r.at[t], tp=(t + i) % Z)
    wo_step(1, 2)
    for i in range(1, Z):
        place = (t + i) % Z
        arrived(stat.at[place], st_r.at[place])
    total = stat[0]
    for i in range(1, Z):
        total += stat[i]
    inv = lax.rsqrt(total / D + epsilon)
    inv = jnp.broadcast_to(inv[0:1], (8, 256))
    both = jnp.where(
        lax.broadcasted_iota(jnp.int32, (8, 256), 0) == 0, inv, inv * inv * inv * total / D
    )
    coef[...] = jnp.concatenate([both] * 16, axis=0).T

    def norm_back(rows, columns, terms_ref):
        return (
            coef[rows, 0:1] * gain[:, columns] * terms_ref[rows, :].astype(F32)
            - li[rows, columns].astype(F32) * coef[rows, 1:2]
        )

    top, bottom = pl.ds(0, 128), pl.ds(128, 128)
    ig_done = pltpu.make_async_copy(ig_out, ig_hbm, res.at[4])
    to_far = [
        rcopy(ig_out.at[r, other], far_in.at[r], one_s.at[i], one_r.at[i], section=1 - s, xh=hp)
        for i, r in ((2, top), (6, bottom))
    ]
    to_keep = rcopy(ig_out.at[:, mine], keep_in, one_s.at[4], one_r.at[4], section=1 - s)
    to_rest = rcopy(ig_out.at[:, other], rest_in, one_s.at[5], one_r.at[5], section=1 - s)
    for copy in to_far + [to_keep, to_rest]:
        sent.append(lambda copy=copy: pl.when(s == 1)(copy.wait_send))

    @pl.when(s == 1)
    def _():
        def down(first, last, columns, terms_ref):
            @pl.loop(first, last)
            def _(i):
                rows = pl.ds(pl.multiple_of(i * 32, 32), 32)
                grad = oc[rows, columns].astype(F32) + mlp[rows, columns].astype(F32)
                ig_out[rows, columns] = (grad + norm_back(rows, columns, terms_ref)).astype(BF16)

        down(0, 4, other, tin)
        to_far[0].start()
        down(4, 8, other, tin)
        to_far[1].start()
        down(0, 8, mine, own_terms)
        to_keep.start()
        to_rest.start()
        ig_done.start()

    wo_step(1, 3)
    arrived(pair.at[t, hp], one_r.at[3])

    def pair_refs(half, first, rows):
        return tuple(
            lambda i, part=pl.ds(start, count): pair.at[i, half, part]
            for start, count in ((first, rows), (first, rows // 2), (first + rows // 2, rows // 2))
        )

    theirs, ours = [pair_refs(hp, 0, 128), pair_refs(hp, 128, 128)], pair_refs(h, 0, 256)

    for n in (0, 1):
        @pl.when(s == 0)
        def _():
            arrived(far_in.at[(top, bottom)[n]], one_r.at[(2, 6)[n]])

            @pl.loop(4 * n, 4 * n + 4)
            def _(i):
                rows = pl.ds(pl.multiple_of(i * 32, 32), 32)
                pair[t, hp, rows, :] = (far_in[rows, :].astype(F32) + pair[t, hp, rows, :].astype(F32)).astype(BF16)

        swap_start(theirs[n][0], gr_s.at[n], gr_r.at[n])

    @pl.when(s == 0)
    def _():
        arrived(keep_in, one_r.at[4])

        @pl.loop(0, 8)
        def _(i):
            rows = pl.ds(pl.multiple_of(i * 32, 32), 32)
            pair[t, h, rows, :] = (keep_in[rows, :].astype(F32) + mlp[rows, mine].astype(F32)).astype(BF16)

    swap_start(ours[0], gr_s.at[2], gr_r.at[2])

    wo_step(2, 0)
    wo_step(2, 1)
    for n in (0, 1):
        swap_near(*theirs[n], gr_s.at[n], gr_r.at[n])
    wo_step(2, 2)

    @pl.when(s == 0)
    def _():
        arrived(rest_in, one_r.at[5])

        def up(columns, terms_ref, from_ref):
            @pl.loop(0, 8)
            def _(i):
                rows = pl.ds(pl.multiple_of(i * 32, 32), 32)
                grad = from_ref[rows, :].astype(F32) + mlp[rows, columns].astype(F32)
                ig_out[rows, columns] = (grad + norm_back(rows, columns, terms_ref)).astype(BF16)

        up(mine, own_terms, keep_in)
        up(other, tin, rest_in)
        ig_done.start()

    for n in (0, 1):
        swap_far(*theirs[n], gr_s.at[n], gr_r.at[n])
    swap_near(*ours, gr_s.at[2], gr_r.at[2])
    wo_step(2, 3)
    swap_far(*ours, gr_s.at[2], gr_r.at[2])
    for n in (0, 1):
        swap_end(theirs[n][0], gr_r.at[n])
    wo_own.wait()
    wo_step(3, 0)

    def product(half, i, columns):
        return lax.dot_general(
            pair[i, half], wo[i, columns, :], (((1,), (1,)), ((), ())), preferred_element_type=F32
        )

    near = [z] + [(z + k) % Z for k in (Z - 1, 1, Z - 2, 2)]

    def first_blocks(half):
        @pl.loop(0, 4)
        def _(n):
            columns = pl.ds(pl.multiple_of(n * 256, 256), 256)
            total = product(half, near[0], columns)
            for i in near[1:]:
                total += product(half, i, columns)
            acc[half, :, columns] = total

    first_blocks(hp)
    wo_step(3, 1)
    swap_end(ours[0], gr_r.at[2])
    first_blocks(h)
    for n in range(4):
        if n > 1:
            wo_step(3, n)
        columns = pl.ds(n * 256, 256)
        for half in (hp, h):
            acc[half, :, columns] += product(half, (z + 3) % Z, columns) + product(half, (z + Z - 3) % Z, columns)
    for j in range(CHUNKS):
        wo_piece(4, j)
        pout[j] = (acc[hp, :, wo_part[j]] + product(hp, far, wo_part[j])).astype(BF16)
        send(pout.at[j], pin.at[j], out_s.at[j], out_r.at[j], xh=hp)
        acc[h, :, wo_part[j]] += product(h, far, wo_part[j])
    results = []
    for j in range(CHUNKS):
        arrived(pin.at[j], out_r.at[j])
        attn[:, wo_part[j]] = (acc[h, :, wo_part[j]] + pin[j].astype(F32)).astype(BF16)
        if j % 2:
            columns = pl.ds((j - 1) * wo_rows, 2 * wo_rows)
            results.append(pltpu.make_async_copy(attn.at[:, columns], attn_out.at[:, columns], res.at[j // 2]))
            results[-1].start()
    for result in results:
        result.wait()
    ig_done.wait()
    finish()


def body(layer_input, norm_gain, kv_cotangent, kv_weight, mlp_grads, output_cotangent, out_weight):
    hbm = pl.BlockSpec(memory_space=pltpu.HBM)
    dma = lambda *n: pltpu.SemaphoreType.DMA(n)
    out = jax.ShapeDtypeStruct((256, 1024), BF16)
    attn, grads = pl.pallas_call(
        kernel,
        out_shape=(out, out),
        in_specs=[hbm] * 7,
        out_specs=(hbm, hbm),
        scratch_shapes=[
            pltpu.VMEM((256, 1024), BF16),
            pltpu.VMEM((256, 1024), BF16),
            pltpu.VMEM((256, 1024), BF16),
            pltpu.VMEM((1, 1024), F32),
            pltpu.VMEM((256, 1024), BF16),
            pltpu.VMEM((256, 1024), BF16),
            pltpu.VMEM((Z, 2, 256, 256), BF16),
            pltpu.VMEM((Z, 256, 512), BF16),
            pltpu.VMEM((Z, 256, 512), BF16),
            pltpu.VMEM((Z, 2, 256, 512), BF16),
            pltpu.VMEM((Z, 1024, 512), BF16),
            pltpu.VMEM((256, 512), F32),
            pltpu.VMEM((256, 512), BF16),
            pltpu.VMEM((256, 512), BF16),
            pltpu.VMEM((256, 512), BF16),
            pltpu.VMEM((256, 512), BF16),
            pltpu.VMEM((256, 512), BF16),
            pltpu.VMEM((256, 512), BF16),
            pltpu.VMEM((Z, 8, 256), F32),
            pltpu.VMEM((256, 128), F32),
            pltpu.VMEM((2, 256, 1024), F32),
            pltpu.VMEM((CHUNKS, 256, 1024 // CHUNKS), BF16),
            pltpu.VMEM((CHUNKS, 256, 1024 // CHUNKS), BF16),
            dma(KV_CHUNKS, 8), dma(KV_CHUNKS, 8),
            dma(KV_CHUNKS, 8), dma(KV_CHUNKS, 8),
            dma(8), dma(8),
            dma(3, 8), dma(3, 8),
            dma(8), dma(8),
            dma(CHUNKS, 8), dma(CHUNKS, 8),
            dma(7), dma(7),
            dma(CHUNKS), dma(CHUNKS),
            dma(7),
            dma(5),
        ],
        compiler_params=pltpu.CompilerParams(
            collective_id=0, has_side_effects=True, vmem_limit_bytes=58 * 2**20
        ),
    )(
        layer_input[0], norm_gain, kv_cotangent[0], kv_weight[0],
        mlp_grads[0], output_cotangent, out_weight[0],
    )
    return attn[None], grads[None]


def solution(mesh):
    fine = Mesh(
        mesh.devices.reshape(mesh.shape["section"], Z, 2, mesh.shape["tp"]),
        ("section", "z", "xh", "tp"),
    )
    in_specs = (
        P("section", SEQ, "tp"),
        P("section", "tp"),
        P("section", SEQ, "tp"),
        P("section", "tp", SEQ),
        P("section", SEQ, "tp"),
        P(SEQ, "tp"),
        P("section", "tp", SEQ),
    )
    out_specs = (P("section", SEQ, "tp"), P("section", SEQ, "tp"))
    return jax.shard_map(body, mesh=fine, in_specs=in_specs, out_specs=out_specs, check_vma=False)
```

```python
import jax
import jax.numpy as jnp
from jax import lax
from jax.experimental import pallas as pl
from jax.experimental.pallas import tpu as pltpu
from jax.sharding import Mesh, PartitionSpec as P

D = 8192
epsilon = 1e-05
SEQ = ("z", "xh")
Z = 8
CHUNKS = 8
KV_CHUNKS = 4
F32, BF16 = jnp.float32, jnp.bfloat16


def rcopy(src, dst, send_sem, recv_sem, **to):
    return pltpu.make_async_remote_copy(
        src_ref=src, dst_ref=dst, send_sem=send_sem, recv_sem=recv_sem,
        device_id=to, device_id_type=pl.DeviceIdType.MESH,
    )


def arrived(ref, sem):
    pltpu.make_async_copy(ref, ref, sem).wait()


def kernel(
    li_hbm, gain_hbm, cot_hbm, kvw_hbm, mlp_hbm, oc_hbm, wo_hbm, result,
       li, gain, mlp, oc, cotb, wz, wk, pair, wo, own_terms, their_terms, tin, give,
    far_in, keep_in, rest_in, stat, coef, acc, pout, pin,
    kv_s, kv_r, a2a_s, a2a_r, cot_s, cot_r, gr_s, gr_r, st_s, st_r, wo_s, wo_r, one_s, one_r, out_s, out_r, loc,
):
    attn, ig_out = result.at[0], result.at[1]
    s, z = lax.axis_index("section"), lax.axis_index("z")
    h, t = lax.axis_index("xh"), lax.axis_index("tp")
    hp = 1 - h
    y, c = t // 2, t % 2
    zr, zl, far = (z + 1) % Z, (z + Z - 1) % Z, (z + 4) % Z
    yr, yl, yo = [((y + i) % 4) * 2 + c for i in (1, 3, 2)]
    core, yr_c, yl_c, yo_c = [i + 1 - 2 * c for i in (t, yr, yl, yo)]
    mine = pl.ds(pl.multiple_of(h * 512, 512), 512)
    other = pl.ds(pl.multiple_of(hp * 512, 512), 512)

    barrier = pltpu.get_barrier_semaphore()
    greet = [{"xh": hp}, {"section": 1 - s}, {"section": 1 - s, "xh": hp}, {"z": zr}, {"z": zl}]
    greet += [{"tp": (t + i) % Z} for i in range(1, Z)]
    for to in greet:
        pl.semaphore_signal(barrier, inc=1, device_id=to, device_id_type=pl.DeviceIdType.MESH)

    loads = [
        pltpu.make_async_copy(src, dst, loc.at[i])
        for i, (src, dst) in enumerate(((li_hbm, li), (gain_hbm, gain), (mlp_hbm, mlp), (oc_hbm, oc)))
    ]
    cot_own = pltpu.make_async_copy(cot_hbm, cotb.at[t, h], loc.at[4])
    wo_own = pltpu.make_async_copy(wo_hbm, wo.at[z], loc.at[5])
    kv_own = pltpu.make_async_copy(kvw_hbm, wz.at[z], loc.at[6])
    for load in [cot_own, kv_own] + loads + [wo_own]:
        load.start()

    pl.semaphore_wait(barrier, len(greet))

    sent = []

    def send(src, dst, send_sem, recv_sem, log=sent, **to):
        copy = rcopy(src, dst, send_sem, recv_sem, **to)
        copy.start()
        log.append(copy.wait_send)

    def finish():
        for wait in sent:
            wait()
        sent.clear()

    def ring_start(own, slot, ss, rs, log=sent):
        send(own, slot(z), ss.at[0], rs.at[0], log, z=zr)
        send(own, slot(z), ss.at[4], rs.at[4], log, z=zl)

    def ring_step(k, slot, rows, ss, rs, log=sent):
        a, b = (z + Z - k) % Z, (z + k) % Z
        first, last = pl.ds(0, rows // 2), pl.ds(rows // 2, rows // 2)
        if k < 4:
            arrived(slot(a), rs.at[k - 1])
            part = slot(a) if k < 3 else slot(a).at[first]
            send(part, part, ss.at[k], rs.at[k], log, z=zr)
            arrived(slot(b), rs.at[k + 3])
            part = slot(b) if k < 3 else slot(b).at[last]
            send(part, part, ss.at[k + 4], rs.at[k + 4], log, z=zl)
        else:
            arrived(slot(a).at[first], rs.at[3])
            arrived(slot(a).at[last], rs.at[7])

    def swap_start(whole, ss, rs):
        own = whole(t)
        send(own, own, ss.at[0], rs.at[0], tp=yr)
        send(own, own, ss.at[1], rs.at[1], tp=yl)
        send(own, own, ss.at[2], rs.at[4], tp=core)

    def swap_near(whole, lower, upper, ss, rs):
        arrived(whole(yl), rs.at[0])
        send(lower(yl), lower(yl), ss.at[3], rs.at[2], tp=yr)
        send(whole(yl), whole(yl), ss.at[4], rs.at[5], tp=core)
        arrived(whole(yr), rs.at[1])
        send(upper(yr), upper(yr), ss.at[5], rs.at[3], tp=yl)
        send(whole(yr), whole(yr), ss.at[6], rs.at[6], tp=core)

    def swap_far(whole, lower, upper, ss, rs):
        arrived(lower(yo), rs.at[2])
        arrived(upper(yo), rs.at[3])
        send(whole(yo), whole(yo), ss.at[7], rs.at[7], tp=core)

    def swap_end(whole, rs):
        for index, place in enumerate((core, yl_c, yr_c, yo_c)):
            arrived(whole(place), rs.at[4 + index])

    kv_rows = 256 // KV_CHUNKS
    kv_part = [pl.ds(j * kv_rows, kv_rows) for j in range(KV_CHUNKS)]

    def kv_start(j):
        own = kvw_hbm.at[kv_part[j]]
        ring_start(own, lambda i: wz.at[i, kv_part[j]], kv_s.at[j], kv_r.at[j])

    def kv_step(k, j):
        ring_step(k, lambda i: wz.at[i, kv_part[j]], kv_rows, kv_s.at[j], kv_r.at[j])

    def pass_on(j):
        land = wk.at[t, kv_part[j]]
        for i in range(1, Z):
            zz = (t + i) % Z
            send(wz.at[zz, kv_part[j]], land, a2a_s.at[j, i], a2a_r.at[j, t], tp=zz)
        pltpu.make_async_copy(wz.at[t, kv_part[j]], land, a2a_r.at[j, t]).start()

    def kv_arrived(j, i):
        arrived(wk.at[i, kv_part[j]], a2a_r.at[j, i])

    wo_rows = 1024 // CHUNKS
    wo_part = [pl.ds(j * wo_rows, wo_rows) for j in range(CHUNKS)]

    wo_sent = [[] for _ in range(CHUNKS)]

    def wo_start(j):
        ring_start(wo_hbm.at[wo_part[j]], lambda i: wo.at[i, wo_part[j]], wo_s.at[j], wo_r.at[j], wo_sent[j])

    def wo_piece(k, j):
        ring_step(k, lambda i: wo.at[i, wo_part[j]], wo_rows, wo_s.at[j], wo_r.at[j], wo_sent[j])

    def wo_step(k, quarter):
        for j in range(quarter * CHUNKS // 4, (quarter + 1) * CHUNKS // 4):
            wo_piece(k, j)

    cot_whole, cot_lower, cot_upper = lambda i: cotb.at[i], lambda i: cotb.at[i, 0], lambda i: cotb.at[i, 1]

    kv_start(0)
    kv_start(1)
    cot_own.wait()
    send(cot_hbm, cotb.at[t, h], one_s.at[0], one_r.at[0], xh=hp)
    for load in loads:
        load.wait()

    @pl.when(s == 1)
    def _():
        @pl.loop(0, 8)
        def _(i):
            rows = pl.ds(pl.multiple_of(i * 32, 32), 32)
            give[rows, :] = (oc[rows, other].astype(F32) + mlp[rows, other].astype(F32)).astype(BF16)

    @pl.when(s == 0)
    def _():
        give[...] = mlp[:, other]

    send(give, pair.at[t, h], one_s.at[3], one_r.at[3], xh=hp)
    kv_step(1, 0)
    kv_step(1, 1)
    kv_start(2)
    arrived(cotb.at[t, hp], one_r.at[0])
    swap_start(cot_whole, cot_s, cot_r)
    kv_step(2, 0)
    kv_step(2, 1)
    kv_step(1, 2)
    kv_step(3, 0)
    kv_step(3, 1)
    kv_start(3)
    swap_near(cot_whole, cot_lower, cot_upper, cot_s, cot_r)
    kv_step(2, 2)
    wo_start(0)
    kv_own.wait()
    kv_step(4, 0)
    pass_on(0)
    kv_step(4, 1)
    pass_on(1)
    kv_step(1, 3)
    wo_start(1)
    kv_step(3, 2)
    swap_far(cot_whole, cot_lower, cot_upper, cot_s, cot_r)
    kv_step(2, 3)
    wo_start(2)
    kv_step(4, 2)
    pass_on(2)
    kv_step(3, 3)
    for j in range(3, CHUNKS):
        wo_start(j)
    kv_step(4, 3)
    pass_on(3)

    @pl.when(s == 1)
    def _():
        @pl.loop(0, 8)
        def _(i):
            rows = pl.ds(pl.multiple_of(i * 32, 32), 32)
            pair[t, h, rows, :] = (oc[rows, mine].astype(F32) + mlp[rows, mine].astype(F32)).astype(BF16)

    @pl.loop(0, 8)
    def _(i):
        rows = pl.ds(pl.multiple_of(i * 32, 32), 32)
        v = li[rows, :].astype(F32)
        coef[rows, :] = jnp.broadcast_to(jnp.sum(v * v, axis=1, keepdims=True), (32, 128))

    swap_end(cot_whole, cot_r)
    for j in range(KV_CHUNKS):
        for i in range(Z):
            kv_arrived(j, i)

    def terms(half, into):
        into[...] = jnp.dot(cotb[0, half], wk[0], preferred_element_type=F32)

        @pl.loop(1, Z)
        def _(i):
            into[...] += jnp.dot(cotb[i, half], wk[i], preferred_element_type=F32)

    terms(hp, own_terms)
    their_terms[...] = own_terms[...].astype(BF16)
    send(their_terms, tin, one_s.at[1], one_r.at[1], xh=hp)
    wo_step(1, 0)
    terms(h, own_terms)
    lane = lax.broadcasted_iota(jnp.int32, (32, 128), 1)
    wo_step(1, 1)
    arrived(tin, one_r.at[1])

    @pl.loop(0, 8)
    def _(i):
        rows = pl.ds(pl.multiple_of(i * 32, 32), 32)
        inner = jnp.sum(gain[:, mine] * own_terms[rows, :] * li[rows, mine].astype(F32), axis=1, keepdims=True)
        inner += jnp.sum(
            gain[:, other] * tin[rows, :].astype(F32) * li[rows, other].astype(F32), axis=1, keepdims=True
        )
        coef[rows, :] = jnp.where(lane == 0, coef[rows, :], jnp.broadcast_to(inner, (32, 128)))

    stat[t] = coef[...].T[:8]
    for i in range(1, Z):
        send(stat.at[t], stat.at[t], st_s.at[i], st_r.at[t], tp=(t + i) % Z)
    wo_step(1, 2)
    for i in range(1, Z):
        place = (t + i) % Z
        arrived(stat.at[place], st_r.at[place])
    total = stat[0]
    for i in range(1, Z):
        total += stat[i]
    inv = lax.rsqrt(total / D + epsilon)
    inv = jnp.broadcast_to(inv[0:1], (8, 256))
    both = jnp.where(
        lax.broadcasted_iota(jnp.int32, (8, 256), 0) == 0, inv, inv * inv * inv * total / D
    )
    coef[...] = jnp.concatenate([both] * 16, axis=0).T

    def norm_back(rows, columns, terms_ref):
        return (
            coef[rows, 0:1] * gain[:, columns] * terms_ref[rows, :].astype(F32)
            - li[rows, columns].astype(F32) * coef[rows, 1:2]
        )

    top, bottom = pl.ds(0, 128), pl.ds(128, 128)
    to_far = [
        rcopy(ig_out.at[r, other], far_in.at[r], one_s.at[i], one_r.at[i], section=1 - s, xh=hp)
        for i, r in ((2, top), (6, bottom))
    ]
    to_keep = rcopy(ig_out.at[:, mine], keep_in, one_s.at[4], one_r.at[4], section=1 - s)
    to_rest = rcopy(ig_out.at[:, other], rest_in, one_s.at[5], one_r.at[5], section=1 - s)
    for copy in to_far + [to_keep, to_rest]:
        sent.append(lambda copy=copy: pl.when(s == 1)(copy.wait_send))

    @pl.when(s == 1)
    def _():
        def down(first, last, columns, terms_ref):
            @pl.loop(first, last)
            def _(i):
                rows = pl.ds(pl.multiple_of(i * 32, 32), 32)
                grad = oc[rows, columns].astype(F32) + mlp[rows, columns].astype(F32)
                ig_out[rows, columns] = (grad + norm_back(rows, columns, terms_ref)).astype(BF16)

        down(0, 4, other, tin)
        to_far[0].start()
        down(4, 8, other, tin)
        to_far[1].start()
        down(0, 8, mine, own_terms)
        to_keep.start()
        to_rest.start()

    wo_step(1, 3)
    arrived(pair.at[t, hp], one_r.at[3])

    def pair_refs(half, first, rows):
        return tuple(
            lambda i, part=pl.ds(start, count): pair.at[i, half, part]
            for start, count in ((first, rows), (first, rows // 2), (first + rows // 2, rows // 2))
        )

    theirs, ours = [pair_refs(hp, 0, 128), pair_refs(hp, 128, 128)], pair_refs(h, 0, 256)

    for n in (0, 1):
        @pl.when(s == 0)
        def _():
            arrived(far_in.at[(top, bottom)[n]], one_r.at[(2, 6)[n]])

            @pl.loop(4 * n, 4 * n + 4)
            def _(i):
                rows = pl.ds(pl.multiple_of(i * 32, 32), 32)
                pair[t, hp, rows, :] = (far_in[rows, :].astype(F32) + pair[t, hp, rows, :].astype(F32)).astype(BF16)

        swap_start(theirs[n][0], gr_s.at[n], gr_r.at[n])

    @pl.when(s == 0)
    def _():
        arrived(keep_in, one_r.at[4])

        @pl.loop(0, 8)
        def _(i):
            rows = pl.ds(pl.multiple_of(i * 32, 32), 32)
            pair[t, h, rows, :] = (keep_in[rows, :].astype(F32) + mlp[rows, mine].astype(F32)).astype(BF16)

    swap_start(ours[0], gr_s.at[2], gr_r.at[2])

    wo_step(2, 0)
    wo_step(2, 1)
    for n in (0, 1):
        swap_near(*theirs[n], gr_s.at[n], gr_r.at[n])
    wo_step(2, 2)

    @pl.when(s == 0)
    def _():
        arrived(rest_in, one_r.at[5])

        def up(columns, terms_ref, from_ref):
            @pl.loop(0, 8)
            def _(i):
                rows = pl.ds(pl.multiple_of(i * 32, 32), 32)
                grad = from_ref[rows, :].astype(F32) + mlp[rows, columns].astype(F32)
                ig_out[rows, columns] = (grad + norm_back(rows, columns, terms_ref)).astype(BF16)

        up(mine, own_terms, keep_in)
        up(other, tin, rest_in)

    for n in (0, 1):
        swap_far(*theirs[n], gr_s.at[n], gr_r.at[n])
    swap_near(*ours, gr_s.at[2], gr_r.at[2])
    wo_step(2, 3)
    swap_far(*ours, gr_s.at[2], gr_r.at[2])
    for n in (0, 1):
        swap_end(theirs[n][0], gr_r.at[n])
    wo_own.wait()
    wo_step(3, 0)

    def product(half, i, columns):
        return lax.dot_general(
            pair[i, half], wo[i, columns, :], (((1,), (1,)), ((), ())), preferred_element_type=F32
        )

    near = [z] + [(z + k) % Z for k in (Z - 1, 1, Z - 2, 2)]

    def first_blocks(half):
        @pl.loop(0, 4)
        def _(n):
            columns = pl.ds(pl.multiple_of(n * 256, 256), 256)
            total = product(half, near[0], columns)
            for i in near[1:]:
                total += product(half, i, columns)
            acc[half, :, columns] = total

    first_blocks(hp)
    wo_step(3, 1)
    swap_end(ours[0], gr_r.at[2])
    first_blocks(h)
    for n in range(4):
        if n > 1:
            wo_step(3, n)
        columns = pl.ds(n * 256, 256)
        for half in (hp, h):
            acc[half, :, columns] += product(half, (z + 3) % Z, columns) + product(half, (z + Z - 3) % Z, columns)
    finish()
    for j in range(CHUNKS):
        wo_piece(4, j)
        pout[j] = (acc[hp, :, wo_part[j]] + product(hp, far, wo_part[j])).astype(BF16)
        send(pout.at[j], pin.at[j], out_s.at[j], out_r.at[j], xh=hp)
        acc[h, :, wo_part[j]] += product(h, far, wo_part[j])
        for wait in wo_sent[j]:
            wait()
    for j in range(CHUNKS):
        arrived(pin.at[j], out_r.at[j])
        attn[:, wo_part[j]] = (acc[h, :, wo_part[j]] + pin[j].astype(F32)).astype(BF16)
    finish()


def body(layer_input, norm_gain, kv_cotangent, kv_weight, mlp_grads, output_cotangent, out_weight):
    hbm = pl.BlockSpec(memory_space=pltpu.HBM)
    dma = lambda *n: pltpu.SemaphoreType.DMA(n)
    out = jax.ShapeDtypeStruct((256, 1024), BF16)
    result = pl.pallas_call(
        kernel,
        out_shape=pltpu.VMEM((2, 256, 1024), BF16),
        in_specs=[hbm] * 7,
        out_specs=pl.BlockSpec(memory_space=pltpu.VMEM),
        scratch_shapes=[
            pltpu.VMEM((256, 1024), BF16),
            pltpu.VMEM((1, 1024), F32),
            pltpu.VMEM((256, 1024), BF16),
            pltpu.VMEM((256, 1024), BF16),
            pltpu.VMEM((Z, 2, 256, 256), BF16),
            pltpu.VMEM((Z, 256, 512), BF16),
            pltpu.VMEM((Z, 256, 512), BF16),
            pltpu.VMEM((Z, 2, 256, 512), BF16),
            pltpu.VMEM((Z, 1024, 512), BF16),
            pltpu.VMEM((256, 512), F32),
            pltpu.VMEM((256, 512), BF16),
            pltpu.VMEM((256, 512), BF16),
            pltpu.VMEM((256, 512), BF16),
            pltpu.VMEM((256, 512), BF16),
            pltpu.VMEM((256, 512), BF16),
            pltpu.VMEM((256, 512), BF16),
            pltpu.VMEM((Z, 8, 256), F32),
            pltpu.VMEM((256, 128), F32),
            pltpu.VMEM((2, 256, 1024), F32),
            pltpu.VMEM((CHUNKS, 256, 1024 // CHUNKS), BF16),
            pltpu.VMEM((CHUNKS, 256, 1024 // CHUNKS), BF16),
            dma(KV_CHUNKS, 8), dma(KV_CHUNKS, 8),
            dma(KV_CHUNKS, 8), dma(KV_CHUNKS, 8),
            dma(8), dma(8),
            dma(3, 8), dma(3, 8),
            dma(8), dma(8),
            dma(CHUNKS, 8), dma(CHUNKS, 8),
            dma(7), dma(7),
            dma(CHUNKS), dma(CHUNKS),
            dma(7),
        ],
        compiler_params=pltpu.CompilerParams(
            collective_id=0, has_side_effects=True, vmem_limit_bytes=58 * 2**20
        ),
    )(
        layer_input[0], norm_gain, kv_cotangent[0], kv_weight[0],
        mlp_grads[0], output_cotangent, out_weight[0],
    )
    return result[:1], result[1:]


def solution(mesh):
    fine = Mesh(
        mesh.devices.reshape(mesh.shape["section"], Z, 2, mesh.shape["tp"]),
        ("section", "z", "xh", "tp"),
    )
    in_specs = (
        P("section", SEQ, "tp"),
        P("section", "tp"),
        P("section", SEQ, "tp"),
        P("section", "tp", SEQ),
        P("section", SEQ, "tp"),
        P(SEQ, "tp"),
        P("section", "tp", SEQ),
    )
    out_specs = (P("section", SEQ, "tp"), P("section", SEQ, "tp"))
    return jax.shard_map(body, mesh=fine, in_specs=in_specs, out_specs=out_specs, check_vma=False)
```

```python
import jax
import jax.numpy as jnp
from jax import lax
from jax.experimental import pallas as pl
from jax.experimental.pallas import tpu as pltpu
from jax.sharding import Mesh, PartitionSpec as P

D = 8192
epsilon = 1e-05
SEQ = ("z", "xh")
Z = 8
CHUNKS = 8
KV_CHUNKS = 4
F32, BF16 = jnp.float32, jnp.bfloat16


def rcopy(src, dst, send_sem, recv_sem, **to):
    return pltpu.make_async_remote_copy(
        src_ref=src, dst_ref=dst, send_sem=send_sem, recv_sem=recv_sem,
        device_id=to, device_id_type=pl.DeviceIdType.MESH,
    )


def arrived(ref, sem):
    pltpu.make_async_copy(ref, ref, sem).wait()


def kernel(
    li_hbm, gain_hbm, cot_hbm, kvw_hbm, mlp_hbm, oc_hbm, wo_hbm, result,
       li, gain, mlp, oc, cotb, wz, wk, pair, wo, own_terms, their_terms, tin, give,
    far_in, keep_in, rest_in, stat, coef, acc, pout, pin,
    kv_s, kv_r, a2a_s, a2a_r, cot_s, cot_r, gr_s, gr_r, st_s, st_r, wo_s, wo_r, one_s, one_r, out_s, out_r, loc,
):
    attn, ig_out = result.at[0], result.at[1]
    s, z = lax.axis_index("section"), lax.axis_index("z")
    h, t = lax.axis_index("xh"), lax.axis_index("tp")
    hp = 1 - h
    y, c = t // 2, t % 2
    zr, zl, far = (z + 1) % Z, (z + Z - 1) % Z, (z + 4) % Z
    yr, yl, yo = [((y + i) % 4) * 2 + c for i in (1, 3, 2)]
    core, yr_c, yl_c, yo_c = [i + 1 - 2 * c for i in (t, yr, yl, yo)]
    mine = pl.ds(pl.multiple_of(h * 512, 512), 512)
    other = pl.ds(pl.multiple_of(hp * 512, 512), 512)

    barrier = pltpu.get_barrier_semaphore()
    greet = [{"xh": hp}, {"section": 1 - s}, {"section": 1 - s, "xh": hp}, {"z": zr}, {"z": zl}]
    greet += [{"tp": (t + i) % Z} for i in range(1, Z)]
    for to in greet:
        pl.semaphore_signal(barrier, inc=1, device_id=to, device_id_type=pl.DeviceIdType.MESH)

    loads = [
        pltpu.make_async_copy(src, dst, loc.at[i])
        for i, (src, dst) in enumerate(((li_hbm, li), (gain_hbm, gain), (mlp_hbm, mlp), (oc_hbm, oc)))
    ]
    cot_own = pltpu.make_async_copy(cot_hbm, cotb.at[t, h], loc.at[4])
    wo_own = pltpu.make_async_copy(wo_hbm, wo.at[z], loc.at[5])
    kv_own = pltpu.make_async_copy(kvw_hbm, wz.at[z], loc.at[6])
    for load in [cot_own, kv_own] + loads + [wo_own]:
        load.start()

    pl.semaphore_wait(barrier, len(greet))

    sent = []

    def send(src, dst, send_sem, recv_sem, log=sent, **to):
        copy = rcopy(src, dst, send_sem, recv_sem, **to)
        copy.start()
        log.append(copy.wait_send)

    def finish():
        for wait in sent:
            wait()
        sent.clear()

    def ring_start(own, slot, ss, rs, log=sent):
        send(own, slot(z), ss.at[0], rs.at[0], log, z=zr)
        send(own, slot(z), ss.at[4], rs.at[4], log, z=zl)

    def ring_step(k, slot, rows, ss, rs, log=sent):
        a, b = (z + Z - k) % Z, (z + k) % Z
        first, last = pl.ds(0, rows // 2), pl.ds(rows // 2, rows // 2)
        if k < 4:
            arrived(slot(a), rs.at[k - 1])
            part = slot(a) if k < 3 else slot(a).at[first]
            send(part, part, ss.at[k], rs.at[k], log, z=zr)
            arrived(slot(b), rs.at[k + 3])
            part = slot(b) if k < 3 else slot(b).at[last]
            send(part, part, ss.at[k + 4], rs.at[k + 4], log, z=zl)
        else:
            arrived(slot(a).at[first], rs.at[3])
            arrived(slot(a).at[last], rs.at[7])

    def swap_start(whole, ss, rs):
        own = whole(t)
        send(own, own, ss.at[0], rs.at[0], tp=yr)
        send(own, own, ss.at[1], rs.at[1], tp=yl)
        send(own, own, ss.at[2], rs.at[4], tp=core)

    def swap_near(whole, lower, upper, ss, rs):
        arrived(whole(yl), rs.at[0])
        send(lower(yl), lower(yl), ss.at[3], rs.at[2], tp=yr)
        send(whole(yl), whole(yl), ss.at[4], rs.at[5], tp=core)
        arrived(whole(yr), rs.at[1])
        send(upper(yr), upper(yr), ss.at[5], rs.at[3], tp=yl)
        send(whole(yr), whole(yr), ss.at[6], rs.at[6], tp=core)

    def swap_far(whole, lower, upper, ss, rs):
        arrived(lower(yo), rs.at[2])
        arrived(upper(yo), rs.at[3])
        send(whole(yo), whole(yo), ss.at[7], rs.at[7], tp=core)

    def swap_end(whole, rs):
        for index, place in enumerate((core, yl_c, yr_c, yo_c)):
            arrived(whole(place), rs.at[4 + index])

    kv_rows = 256 // KV_CHUNKS
    kv_part = [pl.ds(j * kv_rows, kv_rows) for j in range(KV_CHUNKS)]

    def kv_start(j):
        own = kvw_hbm.at[kv_part[j]]
        ring_start(own, lambda i: wz.at[i, kv_part[j]], kv_s.at[j], kv_r.at[j])

    def kv_step(k, j):
        ring_step(k, lambda i: wz.at[i, kv_part[j]], kv_rows, kv_s.at[j], kv_r.at[j])

    def pass_on(j):
        land = wk.at[t, kv_part[j]]
        for i in range(1, Z):
            zz = (t + i) % Z
            send(wz.at[zz, kv_part[j]], land, a2a_s.at[j, i], a2a_r.at[j, t], tp=zz)
        pltpu.make_async_copy(wz.at[t, kv_part[j]], land, a2a_r.at[j, t]).start()

    def kv_arrived(j, i):
        arrived(wk.at[i, kv_part[j]], a2a_r.at[j, i])

    wo_rows = 1024 // CHUNKS
    wo_part = [pl.ds(j * wo_rows, wo_rows) for j in range(CHUNKS)]

    wo_sent = [[] for _ in range(CHUNKS)]

    def wo_start(j):
        ring_start(wo_hbm.at[wo_part[j]], lambda i: wo.at[i, wo_part[j]], wo_s.at[j], wo_r.at[j], wo_sent[j])

    def wo_piece(k, j):
        ring_step(k, lambda i: wo.at[i, wo_part[j]], wo_rows, wo_s.at[j], wo_r.at[j], wo_sent[j])

    def wo_step(k, quarter):
        for j in range(quarter * CHUNKS // 4, (quarter + 1) * CHUNKS // 4):
            wo_piece(k, j)

    cot_whole, cot_lower, cot_upper = lambda i: cotb.at[i], lambda i: cotb.at[i, 0], lambda i: cotb.at[i, 1]

    kv_start(0)
    kv_start(1)
    cot_own.wait()
    send(cot_hbm, cotb.at[t, h], one_s.at[0], one_r.at[0], xh=hp)
    for load in loads:
        load.wait()

    @pl.when(s == 1)
    def _():
        @pl.loop(0, 8)
        def _(i):
            rows = pl.ds(pl.multiple_of(i * 32, 32), 32)
            give[rows, :] = (oc[rows, other].astype(F32) + mlp[rows, other].astype(F32)).astype(BF16)

    @pl.when(s == 0)
    def _():
        give[...] = mlp[:, other]

    send(give, pair.at[t, h], one_s.at[3], one_r.at[3], xh=hp)
    kv_step(1, 0)
    kv_step(1, 1)
    kv_start(2)
    arrived(cotb.at[t, hp], one_r.at[0])
    swap_start(cot_whole, cot_s, cot_r)
    kv_step(2, 0)
    kv_step(2, 1)
    kv_step(1, 2)
    kv_step(3, 0)
    kv_step(3, 1)
    kv_start(3)
    swap_near(cot_whole, cot_lower, cot_upper, cot_s, cot_r)
    kv_step(2, 2)
    wo_start(0)
    wo_start(1)
    kv_own.wait()
    kv_step(4, 0)
    pass_on(0)
    kv_step(4, 1)
    pass_on(1)
    kv_step(1, 3)
    wo_start(2)
    kv_step(3, 2)
    swap_far(cot_whole, cot_lower, cot_upper, cot_s, cot_r)
    kv_step(2, 3)
    wo_start(3)
    wo_start(4)
    kv_step(4, 2)
    pass_on(2)
    kv_step(3, 3)
    for j in range(5, CHUNKS):
        wo_start(j)
    kv_step(4, 3)
    pass_on(3)
    wo_step(1, 0)

    @pl.when(s == 1)
    def _():
        @pl.loop(0, 8)
        def _(i):
            rows = pl.ds(pl.multiple_of(i * 32, 32), 32)
            pair[t, h, rows, :] = (oc[rows, mine].astype(F32) + mlp[rows, mine].astype(F32)).astype(BF16)

    @pl.loop(0, 8)
    def _(i):
        rows = pl.ds(pl.multiple_of(i * 32, 32), 32)
        v = li[rows, :].astype(F32)
        coef[rows, :] = jnp.broadcast_to(jnp.sum(v * v, axis=1, keepdims=True), (32, 128))

    wo_step(1, 1)
    swap_end(cot_whole, cot_r)
    for j in range(KV_CHUNKS):
        for i in range(Z):
            kv_arrived(j, i)

    def terms(half, columns):
        total = jnp.dot(cotb[0, half], wk[0, :, columns], preferred_element_type=F32)
        for i in range(1, Z):
            total += jnp.dot(cotb[i, half], wk[i, :, columns], preferred_element_type=F32)
        return total

    for n, columns in enumerate((pl.ds(0, 256), pl.ds(256, 256))):
        their_terms[:, columns] = terms(hp, columns).astype(BF16)
        index = (1, 7)[n]
        send(their_terms.at[:, columns], tin.at[:, columns], one_s.at[index], one_r.at[index], xh=hp)
    wo_step(1, 2)
    for columns in (pl.ds(0, 256), pl.ds(256, 256)):
        own_terms[:, columns] = terms(h, columns)
    lane = lax.broadcasted_iota(jnp.int32, (32, 128), 1)

    def inner(columns, terms_ref, so_far):
        @pl.loop(0, 8)
        def _(i):
            rows = pl.ds(pl.multiple_of(i * 32, 32), 32)
            part = jnp.sum(
                gain[:, columns] * terms_ref[rows, :].astype(F32) * li[rows, columns].astype(F32),
                axis=1, keepdims=True,
            )
            if so_far:
                part += coef[rows, 1:2]
            coef[rows, :] = jnp.where(lane == 0, coef[rows, :], jnp.broadcast_to(part, (32, 128)))

    inner(mine, own_terms, False)
    wo_step(1, 3)
    for columns, index in ((pl.ds(0, 256), 1), (pl.ds(256, 256), 7)):
        arrived(tin.at[:, columns], one_r.at[index])

    inner(other, tin, True)
    stat[t] = coef[...].T[:8]
    for i in range(1, Z):
        send(stat.at[t], stat.at[t], st_s.at[i], st_r.at[t], tp=(t + i) % Z)
    for i in range(1, Z):
        place = (t + i) % Z
        arrived(stat.at[place], st_r.at[place])
    total = stat[0]
    for i in range(1, Z):
        total += stat[i]
    inv = lax.rsqrt(total / D + epsilon)
    inv = jnp.broadcast_to(inv[0:1], (8, 256))
    both = jnp.where(
        lax.broadcasted_iota(jnp.int32, (8, 256), 0) == 0, inv, inv * inv * inv * total / D
    )
    coef[...] = jnp.concatenate([both] * 16, axis=0).T

    def norm_back(rows, columns, terms_ref):
        return (
            coef[rows, 0:1] * gain[:, columns] * terms_ref[rows, :].astype(F32)
            - li[rows, columns].astype(F32) * coef[rows, 1:2]
        )

    top, bottom = pl.ds(0, 128), pl.ds(128, 128)
    to_far = [
        rcopy(ig_out.at[r, other], far_in.at[r], one_s.at[i], one_r.at[i], section=1 - s, xh=hp)
        for i, r in ((2, top), (6, bottom))
    ]
    to_keep = rcopy(ig_out.at[:, mine], keep_in, one_s.at[4], one_r.at[4], section=1 - s)
    to_rest = rcopy(ig_out.at[:, other], rest_in, one_s.at[5], one_r.at[5], section=1 - s)
    for copy in to_far + [to_keep, to_rest]:
        sent.append(lambda copy=copy: pl.when(s == 1)(copy.wait_send))

    @pl.when(s == 1)
    def _():
        def down(first, last, columns, terms_ref):
            @pl.loop(first, last)
            def _(i):
                rows = pl.ds(pl.multiple_of(i * 32, 32), 32)
                grad = oc[rows, columns].astype(F32) + mlp[rows, columns].astype(F32)
                ig_out[rows, columns] = (grad + norm_back(rows, columns, terms_ref)).astype(BF16)

        down(0, 4, other, tin)
        to_far[0].start()
        down(4, 8, other, tin)
        to_far[1].start()
        down(0, 8, mine, own_terms)
        to_keep.start()
        to_rest.start()

    wo_step(2, 0)
    arrived(pair.at[t, hp], one_r.at[3])

    def pair_refs(half, first, rows):
        return tuple(
            lambda i, part=pl.ds(start, count): pair.at[i, half, part]
            for start, count in ((first, rows), (first, rows // 2), (first + rows // 2, rows // 2))
        )

    theirs, ours = [pair_refs(hp, 0, 128), pair_refs(hp, 128, 128)], pair_refs(h, 0, 256)

    for n in (0, 1):
        @pl.when(s == 0)
        def _():
            arrived(far_in.at[(top, bottom)[n]], one_r.at[(2, 6)[n]])

            @pl.loop(4 * n, 4 * n + 4)
            def _(i):
                rows = pl.ds(pl.multiple_of(i * 32, 32), 32)
                pair[t, hp, rows, :] = (far_in[rows, :].astype(F32) + pair[t, hp, rows, :].astype(F32)).astype(BF16)

        swap_start(theirs[n][0], gr_s.at[n], gr_r.at[n])

    @pl.when(s == 0)
    def _():
        arrived(keep_in, one_r.at[4])

        @pl.loop(0, 8)
        def _(i):
            rows = pl.ds(pl.multiple_of(i * 32, 32), 32)
            pair[t, h, rows, :] = (keep_in[rows, :].astype(F32) + mlp[rows, mine].astype(F32)).astype(BF16)

    swap_start(ours[0], gr_s.at[2], gr_r.at[2])

    wo_step(2, 1)
    for n in (0, 1):
        swap_near(*theirs[n], gr_s.at[n], gr_r.at[n])
    wo_step(2, 2)

    @pl.when(s == 0)
    def _():
        arrived(rest_in, one_r.at[5])

        def up(columns, terms_ref, from_ref):
            @pl.loop(0, 8)
            def _(i):
                rows = pl.ds(pl.multiple_of(i * 32, 32), 32)
                grad = from_ref[rows, :].astype(F32) + mlp[rows, columns].astype(F32)
                ig_out[rows, columns] = (grad + norm_back(rows, columns, terms_ref)).astype(BF16)

        up(mine, own_terms, keep_in)
        up(other, tin, rest_in)

    for n in (0, 1):
        swap_far(*theirs[n], gr_s.at[n], gr_r.at[n])
    swap_near(*ours, gr_s.at[2], gr_r.at[2])
    wo_step(2, 3)
    swap_far(*ours, gr_s.at[2], gr_r.at[2])
    for n in (0, 1):
        swap_end(theirs[n][0], gr_r.at[n])
    wo_own.wait()
    wo_step(3, 0)

    def product(half, i, columns):
        return lax.dot_general(
            pair[i, half], wo[i, columns, :], (((1,), (1,)), ((), ())), preferred_element_type=F32
        )

    near = [z] + [(z + k) % Z for k in (Z - 1, 1, Z - 2, 2)]

    def first_blocks(half):
        @pl.loop(0, 4)
        def _(n):
            columns = pl.ds(pl.multiple_of(n * 256, 256), 256)
            total = product(half, near[0], columns)
            for i in near[1:]:
                total += product(half, i, columns)
            acc[half, :, columns] = total

    first_blocks(hp)
    wo_step(3, 1)
    swap_end(ours[0], gr_r.at[2])
    first_blocks(h)
    for n in range(4):
        if n > 1:
            wo_step(3, n)
        columns = pl.ds(n * 256, 256)
        for half in (hp, h):
            acc[half, :, columns] += product(half, (z + 3) % Z, columns) + product(half, (z + Z - 3) % Z, columns)
    finish()
    for j in range(CHUNKS):
        wo_piece(4, j)
        pout[j] = (acc[hp, :, wo_part[j]] + product(hp, far, wo_part[j])).astype(BF16)
        send(pout.at[j], pin.at[j], out_s.at[j], out_r.at[j], xh=hp)
        acc[h, :, wo_part[j]] += product(h, far, wo_part[j])
        for wait in wo_sent[j]:
            wait()
    for j in range(CHUNKS):
        arrived(pin.at[j], out_r.at[j])
        attn[:, wo_part[j]] = (acc[h, :, wo_part[j]] + pin[j].astype(F32)).astype(BF16)
    finish()


def body(layer_input, norm_gain, kv_cotangent, kv_weight, mlp_grads, output_cotangent, out_weight):
    hbm = pl.BlockSpec(memory_space=pltpu.HBM)
    dma = lambda *n: pltpu.SemaphoreType.DMA(n)
    out = jax.ShapeDtypeStruct((256, 1024), BF16)
    result = pl.pallas_call(
        kernel,
        out_shape=pltpu.VMEM((2, 256, 1024), BF16),
        in_specs=[hbm] * 7,
        out_specs=pl.BlockSpec(memory_space=pltpu.VMEM),
        scratch_shapes=[
            pltpu.VMEM((256, 1024), BF16),
            pltpu.VMEM((1, 1024), F32),
            pltpu.VMEM((256, 1024), BF16),
            pltpu.VMEM((256, 1024), BF16),
            pltpu.VMEM((Z, 2, 256, 256), BF16),
            pltpu.VMEM((Z, 256, 512), BF16),
            pltpu.VMEM((Z, 256, 512), BF16),
            pltpu.VMEM((Z, 2, 256, 512), BF16),
            pltpu.VMEM((Z, 1024, 512), BF16),
            pltpu.VMEM((256, 512), F32),
            pltpu.VMEM((256, 512), BF16),
            pltpu.VMEM((256, 512), BF16),
            pltpu.VMEM((256, 512), BF16),
            pltpu.VMEM((256, 512), BF16),
            pltpu.VMEM((256, 512), BF16),
            pltpu.VMEM((256, 512), BF16),
            pltpu.VMEM((Z, 8, 256), F32),
            pltpu.VMEM((256, 128), F32),
            pltpu.VMEM((2, 256, 1024), F32),
            pltpu.VMEM((CHUNKS, 256, 1024 // CHUNKS), BF16),
            pltpu.VMEM((CHUNKS, 256, 1024 // CHUNKS), BF16),
            dma(KV_CHUNKS, 8), dma(KV_CHUNKS, 8),
            dma(KV_CHUNKS, 8), dma(KV_CHUNKS, 8),
            dma(8), dma(8),
            dma(3, 8), dma(3, 8),
            dma(8), dma(8),
            dma(CHUNKS, 8), dma(CHUNKS, 8),
            dma(8), dma(8),
            dma(CHUNKS), dma(CHUNKS),
            dma(7),
        ],
        compiler_params=pltpu.CompilerParams(
            collective_id=0, has_side_effects=True, vmem_limit_bytes=58 * 2**20
        ),
    )(
        layer_input[0], norm_gain, kv_cotangent[0], kv_weight[0],
        mlp_grads[0], output_cotangent, out_weight[0],
    )
    return result[:1], result[1:]


def solution(mesh):
    fine = Mesh(
        mesh.devices.reshape(mesh.shape["section"], Z, 2, mesh.shape["tp"]),
        ("section", "z", "xh", "tp"),
    )
    in_specs = (
        P("section", SEQ, "tp"),
        P("section", "tp"),
        P("section", SEQ, "tp"),
        P("section", "tp", SEQ),
        P("section", SEQ, "tp"),
        P(SEQ, "tp"),
        P("section", "tp", SEQ),
    )
    out_specs = (P("section", SEQ, "tp"), P("section", SEQ, "tp"))
    return jax.shard_map(body, mesh=fine, in_specs=in_specs, out_specs=out_specs, check_vma=False)
```

```python
import jax
import jax.numpy as jnp
from jax import lax
from jax.experimental import pallas as pl
from jax.experimental.pallas import tpu as pltpu
from jax.sharding import Mesh, PartitionSpec as P

D = 8192
epsilon = 1e-05
SEQ = ("z", "xh")
Z = 8
CHUNKS = 8
KV_CHUNKS = 4
F32, BF16 = jnp.float32, jnp.bfloat16


def rcopy(src, dst, send_sem, recv_sem, **to):
    return pltpu.make_async_remote_copy(
        src_ref=src, dst_ref=dst, send_sem=send_sem, recv_sem=recv_sem,
        device_id=to, device_id_type=pl.DeviceIdType.MESH,
    )


def arrived(ref, sem):
    pltpu.make_async_copy(ref, ref, sem).wait()


def kernel(
    li_hbm, gain_hbm, cot_hbm, kvw_hbm, mlp_hbm, oc_hbm, wo_hbm, result,
       li, gain, mlp, oc, cotb, wz, wk, pair, wo, own_terms, their_terms, tin, give,
    far_in, keep_in, rest_in, stat, coef, acc, pout, pin,
    kv_s, kv_r, a2a_s, a2a_r, cot_s, cot_r, gr_s, gr_r, st_s, st_r, wo_s, wo_r, one_s, one_r, out_s, out_r, loc,
):
    attn, ig_out = result.at[0], result.at[1]
    s, z = lax.axis_index("section"), lax.axis_index("z")
    h, t = lax.axis_index("xh"), lax.axis_index("tp")
    hp = 1 - h
    y, c = t // 2, t % 2
    zr, zl, far = (z + 1) % Z, (z + Z - 1) % Z, (z + 4) % Z
    yr, yl, yo = [((y + i) % 4) * 2 + c for i in (1, 3, 2)]
    core, yr_c, yl_c, yo_c = [i + 1 - 2 * c for i in (t, yr, yl, yo)]
    mine = pl.ds(pl.multiple_of(h * 512, 512), 512)
    other = pl.ds(pl.multiple_of(hp * 512, 512), 512)

    barrier = pltpu.get_barrier_semaphore()
    greet = [{"xh": hp}, {"section": 1 - s}, {"section": 1 - s, "xh": hp}, {"z": zr}, {"z": zl}]
    greet += [{"tp": (t + i) % Z} for i in range(1, Z)]
    for to in greet:
        pl.semaphore_signal(barrier, inc=1, device_id=to, device_id_type=pl.DeviceIdType.MESH)

    loads = [
        pltpu.make_async_copy(src, dst, loc.at[i])
        for i, (src, dst) in enumerate(((li_hbm, li), (gain_hbm, gain), (mlp_hbm, mlp), (oc_hbm, oc)))
    ]
    cot_own = pltpu.make_async_copy(cot_hbm, cotb.at[t, h], loc.at[4])
    wo_own = pltpu.make_async_copy(wo_hbm, wo.at[z], loc.at[5])
    kv_own = pltpu.make_async_copy(kvw_hbm, wz.at[z], loc.at[6])
    for load in [cot_own, kv_own] + loads + [wo_own]:
        load.start()

    pl.semaphore_wait(barrier, len(greet))

    sent = []

    def send(src, dst, send_sem, recv_sem, log=sent, **to):
        copy = rcopy(src, dst, send_sem, recv_sem, **to)
        copy.start()
        log.append(copy.wait_send)

    def finish():
        for wait in sent:
            wait()
        sent.clear()

    def ring_start(own, slot, ss, rs, log=sent):
        send(own, slot(z), ss.at[0], rs.at[0], log, z=zr)
        send(own, slot(z), ss.at[4], rs.at[4], log, z=zl)

    def ring_step(k, slot, rows, ss, rs, log=sent):
        a, b = (z + Z - k) % Z, (z + k) % Z
        first, last = pl.ds(0, rows // 2), pl.ds(rows // 2, rows // 2)
        if k < 4:
            arrived(slot(a), rs.at[k - 1])
            part = slot(a) if k < 3 else slot(a).at[first]
            send(part, part, ss.at[k], rs.at[k], log, z=zr)
            arrived(slot(b), rs.at[k + 3])
            part = slot(b) if k < 3 else slot(b).at[last]
            send(part, part, ss.at[k + 4], rs.at[k + 4], log, z=zl)
        else:
            arrived(slot(a).at[first], rs.at[3])
            arrived(slot(a).at[last], rs.at[7])

    def swap_start(whole, ss, rs):
        own = whole(t)
        send(own, own, ss.at[0], rs.at[0], tp=yr)
        send(own, own, ss.at[1], rs.at[1], tp=yl)
        send(own, own, ss.at[2], rs.at[4], tp=core)

    def swap_near(whole, lower, upper, ss, rs):
        arrived(whole(yl), rs.at[0])
        send(lower(yl), lower(yl), ss.at[3], rs.at[2], tp=yr)
        send(whole(yl), whole(yl), ss.at[4], rs.at[5], tp=core)
        arrived(whole(yr), rs.at[1])
        send(upper(yr), upper(yr), ss.at[5], rs.at[3], tp=yl)
        send(whole(yr), whole(yr), ss.at[6], rs.at[6], tp=core)

    def swap_far(whole, lower, upper, ss, rs):
        arrived(lower(yo), rs.at[2])
        arrived(upper(yo), rs.at[3])
        send(whole(yo), whole(yo), ss.at[7], rs.at[7], tp=core)

    def swap_end(whole, rs):
        for index, place in enumerate((core, yl_c, yr_c, yo_c)):
            arrived(whole(place), rs.at[4 + index])

    kv_rows = 256 // KV_CHUNKS
    kv_part = [pl.ds(j * kv_rows, kv_rows) for j in range(KV_CHUNKS)]

    def kv_start(j):
        own = kvw_hbm.at[kv_part[j]]
        ring_start(own, lambda i: wz.at[i, kv_part[j]], kv_s.at[j], kv_r.at[j])

    def kv_step(k, j):
        ring_step(k, lambda i: wz.at[i, kv_part[j]], kv_rows, kv_s.at[j], kv_r.at[j])

    def pass_on(j):
        land = wk.at[t, kv_part[j]]
        for i in range(1, Z):
            zz = (t + i) % Z
            send(wz.at[zz, kv_part[j]], land, a2a_s.at[j, i], a2a_r.at[j, t], tp=zz)
        pltpu.make_async_copy(wz.at[t, kv_part[j]], land, a2a_r.at[j, t]).start()

    def kv_arrived(j, i):
        arrived(wk.at[i, kv_part[j]], a2a_r.at[j, i])

    wo_rows = 1024 // CHUNKS
    wo_part = [pl.ds(j * wo_rows, wo_rows) for j in range(CHUNKS)]

    wo_sent = [[] for _ in range(CHUNKS)]

    def wo_start(j):
        ring_start(wo_hbm.at[wo_part[j]], lambda i: wo.at[i, wo_part[j]], wo_s.at[j], wo_r.at[j], wo_sent[j])

    def wo_piece(k, j):
        ring_step(k, lambda i: wo.at[i, wo_part[j]], wo_rows, wo_s.at[j], wo_r.at[j], wo_sent[j])

    def wo_step(k, quarter):
        for j in range(quarter * CHUNKS // 4, (quarter + 1) * CHUNKS // 4):
            wo_piece(k, j)

    cot_whole, cot_lower, cot_upper = lambda i: cotb.at[i], lambda i: cotb.at[i, 0], lambda i: cotb.at[i, 1]

    kv_start(0)
    kv_start(1)
    cot_own.wait()
    send(cot_hbm, cotb.at[t, h], one_s.at[0], one_r.at[0], xh=hp)
    for load in loads:
        load.wait()

    @pl.when(s == 1)
    def _():
        @pl.loop(0, 8)
        def _(i):
            rows = pl.ds(pl.multiple_of(i * 32, 32), 32)
            give[rows, :] = (oc[rows, other].astype(F32) + mlp[rows, other].astype(F32)).astype(BF16)

    @pl.when(s == 0)
    def _():
        give[...] = mlp[:, other]

    send(give, pair.at[t, h], one_s.at[3], one_r.at[3], xh=hp)
    kv_step(1, 0)
    kv_step(1, 1)
    kv_start(2)
    arrived(cotb.at[t, hp], one_r.at[0])
    swap_start(cot_whole, cot_s, cot_r)
    kv_step(2, 0)
    kv_step(2, 1)
    kv_step(1, 2)
    kv_step(3, 0)
    kv_step(3, 1)
    kv_start(3)
    swap_near(cot_whole, cot_lower, cot_upper, cot_s, cot_r)
    kv_step(2, 2)
    wo_start(0)
    wo_start(1)
    kv_own.wait()
    kv_step(4, 0)
    pass_on(0)
    kv_step(4, 1)
    pass_on(1)
    kv_step(1, 3)
    wo_start(2)
    kv_step(3, 2)
    swap_far(cot_whole, cot_lower, cot_upper, cot_s, cot_r)
    kv_step(2, 3)
    wo_start(3)
    wo_start(4)
    kv_step(4, 2)
    pass_on(2)
    kv_step(3, 3)
    for j in range(5, CHUNKS):
        wo_start(j)
    kv_step(4, 3)
    pass_on(3)
    wo_step(1, 0)

    @pl.when(s == 1)
    def _():
        @pl.loop(0, 8)
        def _(i):
            rows = pl.ds(pl.multiple_of(i * 32, 32), 32)
            pair[t, h, rows, :] = (oc[rows, mine].astype(F32) + mlp[rows, mine].astype(F32)).astype(BF16)

    @pl.loop(0, 8)
    def _(i):
        rows = pl.ds(pl.multiple_of(i * 32, 32), 32)
        v = li[rows, :].astype(F32)
        coef[rows, :] = jnp.broadcast_to(jnp.sum(v * v, axis=1, keepdims=True), (32, 128))

    wo_step(1, 1)
    swap_end(cot_whole, cot_r)
    for j in range(KV_CHUNKS):
        for i in range(Z):
            kv_arrived(j, i)

    def terms(half, columns):
        total = jnp.dot(cotb[0, half], wk[0, :, columns], preferred_element_type=F32)
        for i in range(1, Z):
            total += jnp.dot(cotb[i, half], wk[i, :, columns], preferred_element_type=F32)
        return total

    for n, columns in enumerate((pl.ds(0, 256), pl.ds(256, 256))):
        their_terms[:, columns] = terms(hp, columns).astype(BF16)
        index = (1, 7)[n]
        send(their_terms.at[:, columns], tin.at[:, columns], one_s.at[index], one_r.at[index], xh=hp)
    wo_step(1, 2)
    for columns in (pl.ds(0, 256), pl.ds(256, 256)):
        own_terms[:, columns] = terms(h, columns)
    lane = lax.broadcasted_iota(jnp.int32, (32, 128), 1)

    def inner(columns, terms_ref, so_far):
        @pl.loop(0, 8)
        def _(i):
            rows = pl.ds(pl.multiple_of(i * 32, 32), 32)
            part = jnp.sum(
                gain[:, columns] * terms_ref[rows, :].astype(F32) * li[rows, columns].astype(F32),
                axis=1, keepdims=True,
            )
            if so_far:
                part += coef[rows, 1:2]
            coef[rows, :] = jnp.where(lane == 0, coef[rows, :], jnp.broadcast_to(part, (32, 128)))

    inner(mine, own_terms, False)
    wo_step(1, 3)
    for columns, index in ((pl.ds(0, 256), 1), (pl.ds(256, 256), 7)):
        arrived(tin.at[:, columns], one_r.at[index])

    inner(other, tin, True)
    stat[t] = coef[...].T[:8]
    for i in range(1, Z):
        send(stat.at[t], stat.at[t], st_s.at[i], st_r.at[t], tp=(t + i) % Z)
    for i in range(1, Z):
        place = (t + i) % Z
        arrived(stat.at[place], st_r.at[place])
    total = stat[0]
    for i in range(1, Z):
        total += stat[i]
    inv = lax.rsqrt(total / D + epsilon)
    inv = jnp.broadcast_to(inv[0:1], (8, 256))
    both = jnp.where(
        lax.broadcasted_iota(jnp.int32, (8, 256), 0) == 0, inv, inv * inv * inv * total / D
    )
    coef[...] = jnp.concatenate([both] * 16, axis=0).T

    def norm_back(rows, columns, terms_ref):
        return (
            coef[rows, 0:1] * gain[:, columns] * terms_ref[rows, :].astype(F32)
            - li[rows, columns].astype(F32) * coef[rows, 1:2]
        )

    top, bottom = pl.ds(0, 128), pl.ds(128, 128)
    to_far = [
        rcopy(ig_out.at[r, other], far_in.at[r], one_s.at[i], one_r.at[i], section=1 - s, xh=hp)
        for i, r in ((2, top), (6, bottom))
    ]
    to_keep = rcopy(ig_out.at[:, mine], keep_in, one_s.at[4], one_r.at[4], section=1 - s)
    to_rest = rcopy(ig_out.at[:, other], rest_in, one_s.at[5], one_r.at[5], section=1 - s)
    for copy in to_far + [to_keep, to_rest]:
        wo_sent[0].append(lambda copy=copy: pl.when(s == 1)(copy.wait_send))

    @pl.when(s == 1)
    def _():
        def down(first, last, columns, terms_ref):
            @pl.loop(first, last)
            def _(i):
                rows = pl.ds(pl.multiple_of(i * 32, 32), 32)
                grad = oc[rows, columns].astype(F32) + mlp[rows, columns].astype(F32)
                ig_out[rows, columns] = (grad + norm_back(rows, columns, terms_ref)).astype(BF16)

        down(0, 4, other, tin)
        to_far[0].start()
        down(4, 8, other, tin)
        to_far[1].start()
        down(0, 8, mine, own_terms)
        to_keep.start()
        to_rest.start()

    wo_step(2, 0)
    finish()
    arrived(pair.at[t, hp], one_r.at[3])

    def pair_refs(half, first, rows):
        return tuple(
            lambda i, part=pl.ds(start, count): pair.at[i, half, part]
            for start, count in ((first, rows), (first, rows // 2), (first + rows // 2, rows // 2))
        )

    theirs, ours = [pair_refs(hp, 0, 128), pair_refs(hp, 128, 128)], pair_refs(h, 0, 256)

    for n in (0, 1):
        @pl.when(s == 0)
        def _():
            arrived(far_in.at[(top, bottom)[n]], one_r.at[(2, 6)[n]])

            @pl.loop(4 * n, 4 * n + 4)
            def _(i):
                rows = pl.ds(pl.multiple_of(i * 32, 32), 32)
                pair[t, hp, rows, :] = (far_in[rows, :].astype(F32) + pair[t, hp, rows, :].astype(F32)).astype(BF16)

        swap_start(theirs[n][0], gr_s.at[n], gr_r.at[n])

    @pl.when(s == 0)
    def _():
        arrived(keep_in, one_r.at[4])

        @pl.loop(0, 8)
        def _(i):
            rows = pl.ds(pl.multiple_of(i * 32, 32), 32)
            pair[t, h, rows, :] = (keep_in[rows, :].astype(F32) + mlp[rows, mine].astype(F32)).astype(BF16)

    swap_start(ours[0], gr_s.at[2], gr_r.at[2])

    wo_step(2, 1)
    for n in (0, 1):
        swap_near(*theirs[n], gr_s.at[n], gr_r.at[n])
    wo_step(2, 2)

    @pl.when(s == 0)
    def _():
        arrived(rest_in, one_r.at[5])

        def up(columns, terms_ref, from_ref):
            @pl.loop(0, 8)
            def _(i):
                rows = pl.ds(pl.multiple_of(i * 32, 32), 32)
                grad = from_ref[rows, :].astype(F32) + mlp[rows, columns].astype(F32)
                ig_out[rows, columns] = (grad + norm_back(rows, columns, terms_ref)).astype(BF16)

        up(mine, own_terms, keep_in)
        up(other, tin, rest_in)

    for n in (0, 1):
        swap_far(*theirs[n], gr_s.at[n], gr_r.at[n])
    swap_near(*ours, gr_s.at[2], gr_r.at[2])
    wo_step(2, 3)
    swap_far(*ours, gr_s.at[2], gr_r.at[2])
    for n in (0, 1):
        swap_end(theirs[n][0], gr_r.at[n])
    wo_own.wait()
    wo_step(3, 0)

    def product(half, i, columns):
        return lax.dot_general(
            pair[i, half], wo[i, columns, :], (((1,), (1,)), ((), ())), preferred_element_type=F32
        )

    near = [z] + [(z + k) % Z for k in (Z - 1, 1, Z - 2, 2)]

    def first_blocks(half):
        @pl.loop(0, 4)
        def _(n):
            columns = pl.ds(pl.multiple_of(n * 256, 256), 256)
            total = product(half, near[0], columns)
            for i in near[1:]:
                total += product(half, i, columns)
            acc[half, :, columns] = total

    first_blocks(hp)
    wo_step(3, 1)
    swap_end(ours[0], gr_r.at[2])
    first_blocks(h)
    for n in range(4):
        if n > 1:
            wo_step(3, n)
        columns = pl.ds(n * 256, 256)
        for half in (hp, h):
            acc[half, :, columns] += product(half, (z + 3) % Z, columns) + product(half, (z + Z - 3) % Z, columns)
    finish()
    for j in range(CHUNKS):
        wo_piece(4, j)
        pout[j] = (acc[hp, :, wo_part[j]] + product(hp, far, wo_part[j])).astype(BF16)
        send(pout.at[j], pin.at[j], out_s.at[j], out_r.at[j], xh=hp)
        acc[h, :, wo_part[j]] += product(h, far, wo_part[j])
        for wait in wo_sent[j]:
            wait()
    for j in range(CHUNKS):
        arrived(pin.at[j], out_r.at[j])
        attn[:, wo_part[j]] = (acc[h, :, wo_part[j]] + pin[j].astype(F32)).astype(BF16)
    finish()


def body(layer_input, norm_gain, kv_cotangent, kv_weight, mlp_grads, output_cotangent, out_weight):
    hbm = pl.BlockSpec(memory_space=pltpu.HBM)
    dma = lambda *n: pltpu.SemaphoreType.DMA(n)
    out = jax.ShapeDtypeStruct((256, 1024), BF16)
    result = pl.pallas_call(
        kernel,
        out_shape=pltpu.VMEM((2, 256, 1024), BF16),
        in_specs=[hbm] * 7,
        out_specs=pl.BlockSpec(memory_space=pltpu.VMEM),
        scratch_shapes=[
            pltpu.VMEM((256, 1024), BF16),
            pltpu.VMEM((1, 1024), F32),
            pltpu.VMEM((256, 1024), BF16),
            pltpu.VMEM((256, 1024), BF16),
            pltpu.VMEM((Z, 2, 256, 256), BF16),
            pltpu.VMEM((Z, 256, 512), BF16),
            pltpu.VMEM((Z, 256, 512), BF16),
            pltpu.VMEM((Z, 2, 256, 512), BF16),
            pltpu.VMEM((Z, 1024, 512), BF16),
            pltpu.VMEM((256, 512), F32),
            pltpu.VMEM((256, 512), BF16),
            pltpu.VMEM((256, 512), BF16),
            pltpu.VMEM((256, 512), BF16),
            pltpu.VMEM((256, 512), BF16),
            pltpu.VMEM((256, 512), BF16),
            pltpu.VMEM((256, 512), BF16),
            pltpu.VMEM((Z, 8, 256), F32),
            pltpu.VMEM((256, 128), F32),
            pltpu.VMEM((2, 256, 1024), F32),
            pltpu.VMEM((CHUNKS, 256, 1024 // CHUNKS), BF16),
            pltpu.VMEM((CHUNKS, 256, 1024 // CHUNKS), BF16),
            dma(KV_CHUNKS, 8), dma(KV_CHUNKS, 8),
            dma(KV_CHUNKS, 8), dma(KV_CHUNKS, 8),
            dma(8), dma(8),
            dma(3, 8), dma(3, 8),
            dma(8), dma(8),
            dma(CHUNKS, 8), dma(CHUNKS, 8),
            dma(8), dma(8),
            dma(CHUNKS), dma(CHUNKS),
            dma(7),
        ],
        compiler_params=pltpu.CompilerParams(
            collective_id=0, has_side_effects=True, vmem_limit_bytes=58 * 2**20
        ),
    )(
        layer_input[0], norm_gain, kv_cotangent[0], kv_weight[0],
        mlp_grads[0], output_cotangent, out_weight[0],
    )
    return result[:1], result[1:]


def solution(mesh):
    fine = Mesh(
        mesh.devices.reshape(mesh.shape["section"], Z, 2, mesh.shape["tp"]),
        ("section", "z", "xh", "tp"),
    )
    in_specs = (
        P("section", SEQ, "tp"),
        P("section", "tp"),
        P("section", SEQ, "tp"),
        P("section", "tp", SEQ),
        P("section", SEQ, "tp"),
        P(SEQ, "tp"),
        P("section", "tp", SEQ),
    )
    out_specs = (P("section", SEQ, "tp"), P("section", SEQ, "tp"))
    return jax.shard_map(body, mesh=fine, in_specs=in_specs, out_specs=out_specs, check_vma=False)
```
